32 devices in a mesh: dp: 8 (over z, x), blk: 4 (over y, core).
Axes of the slice: x: 2, y: 2, z: 4, core: 2. Of those that a mesh axis runs over, the one named last changes fastest.
Arguments:
- tokens: bfloat16 [64, 512, 768], P('dp', 'blk'), may hold values from -6 to 6
- fragments: int32 [64, 512], P('dp', 'blk'), may hold values from 0 to 511, as said below
- cotangent: bfloat16 [64, 512, 768], P('dp', 'blk'), may hold values from -6 to 6
- query_weight: bfloat16 [768, 768], P('dp'), may hold values from -0.21875 to 0.21875
- query_bias: bfloat16 [768], P('dp'), may hold values from -1.75 to 1.75
- key_weight: bfloat16 [768, 768], P('dp'), may hold values from -0.21875 to 0.21875
- value_weight: bfloat16 [768, 768], P('dp'), may hold values from -0.21875 to 0.21875
- value_bias: bfloat16 [768], P('dp'), may hold values from -1.75 to 1.75
- out_weight: bfloat16 [768, 768], P('dp'), may hold values from -1.25 to 1.25
- out_bias: bfloat16 [768], P('dp'), may hold values from -1.75 to 1.75
- first_gain: bfloat16 [768], P('dp'), may hold values from 0.5 to 1.5
- first_shift: bfloat16 [768], P('dp'), may hold values from -1.75 to 1.75
- up_weight: bfloat16 [768, 3072], P('dp'), may hold values from -0.21875 to 0.21875
- up_bias: bfloat16 [3072], P('dp'), may hold values from -1.75 to 1.75
- down_weight: bfloat16 [3072, 768], P('dp'), may hold values from -0.109375 to 0.109375
- down_bias: bfloat16 [768], P('dp'), may hold values from -1.75 to 1.75
- second_gain: bfloat16 [768], P('dp'), may hold values from 0.5 to 1.5
- second_shift: bfloat16 [768], P('dp'), may hold values from -1.75 to 1.75
Outputs:
- output: bfloat16 [64, 512, 768], P('dp', 'blk')
- grad_tokens: bfloat16 [64, 512, 768], P('dp', 'blk')
- query_weight_gradient: float32 [768, 768], P('dp')
- grad_query_bias: float32 [768], P('dp')
- grad_key_weight: float32 [768, 768], P('dp')
- grad_value_weight: float32 [768, 768], P('dp')
- grad_value_bias: float32 [768], P('dp')
- grad_out_weight: float32 [768, 768], P('dp')
- grad_out_bias: float32 [768], P('dp')
- grad_first_gain: float32 [768], P('dp')
- grad_first_shift: float32 [768], P('dp')
- grad_up_weight: float32 [768, 3072], P('dp')
- grad_up_bias: float32 [3072], P('dp')
- grad_down_weight: float32 [3072, 768], P('dp')
- grad_down_bias: float32 [768], P('dp')
- grad_second_gain: float32 [768], P('dp')
- grad_second_shift: float32 [768], P('dp')
The draws below stay inside these ranges and needn't reach their ends.
Inputs may be any that keep to these rules, and one draw needn't show every extreme that they name: `fragments`: fragment ids never fall along a row; the last position of every row is a fragment of its own with id 512 - 1.
All inputs are finite; a program needn't handle non-finite values.
Results may differ from the reference program's by a relative error of at most 0.024.
Values may be sent and summed in bfloat16 or wider, within the bound.
No kernel may reach another device: no remote copies, remote signals or barrier semaphores. Data moves between devices by JAX's collectives and lax.ppermute only.
A program may use at most 256 MiB of HBM per device.

```python
import math
import jax
import jax.numpy as jnp
from jax import lax

D = 768
H = 12
DH = 64
FF = 3072
SEQS = 4
STRETCH = 128
LEN = 512
ROWS = 64


def draw_fragments(key, part):
    key = jax.random.fold_in(key, 11)
    key_breaks, key_pick, key_head, key_tail = jax.random.split(key, 4)
    positions = jnp.arange(LEN)
    breaks = jax.random.randint(key_breaks, (ROWS, LEN), 0, STRETCH + STRETCH // 4) == 0
    breaks = breaks & (positions[None, :] > 0)
    spread_ids = jnp.cumsum(breaks.astype(jnp.int32), axis=1)
    group_count = ROWS // SEQS
    picked = jax.random.randint(key_pick, (group_count,), 0, SEQS)
    chosen = (jnp.arange(SEQS)[None, :] == picked[:, None]).reshape(ROWS)
    head_end = jax.random.randint(key_head, (ROWS, 1), 0, STRETCH // 2)
    tail_start = LEN - jax.random.randint(key_tail, (ROWS, 1), 0, STRETCH // 2)
    span_ids = (positions[None, :] >= head_end).astype(jnp.int32) + (positions[None, :] >= tail_start).astype(jnp.int32)
    ids = jnp.where(chosen[:, None], span_ids, spread_ids)
    ids = jnp.where(positions[None, :] == LEN - 1, LEN - 1, ids)
    return ids.astype(jnp.int32)


def spiked(values, key, source, target, shards_of, factor):
    owner, partner = [(jnp.arange(values.shape[dim]) // (values.shape[dim] // shards_of)).reshape([-1 if axis == dim else 1 for axis in range(values.ndim)]) for dim in (source, target)]
    chosen = jax.random.permutation(key, shards_of)[partner]
    strong = (owner == chosen) | (owner == (partner + shards_of // 2) % shards_of)
    return jnp.where(strong, factor * values, values)


def shard_levels(rng, extent, shards, smallest, top_value):
    level = 1.0
    for axis_at, parts in shards:
        heights = jax.random.uniform(jax.random.fold_in(jax.random.fold_in(rng, 6), axis_at), (parts,), jnp.float32, smallest / len(shards), top_value / len(shards))
        level = level * jnp.repeat(jnp.exp(heights), extent[axis_at] // parts).reshape((-1,) + (1,) * (len(extent) - 1 - axis_at))
    return level


def normal_values(rng, extent, deviation, most, pieces=(), kind=jnp.bfloat16):
    level = shard_levels(rng, extent, pieces, -0.22, 0.18) if pieces else 1.0
    values = jax.random.normal(rng, extent, jnp.float32) * deviation * level
    return jnp.minimum(jnp.maximum(values, -most), most).astype(kind)


def gaussian_with(key, dims, scale, most, shards, heavy, dtype=jnp.bfloat16):
    entries = scale * jax.random.normal(key, dims, jnp.float32)
    if shards:
        entries = entries * shard_levels(key, dims, shards, -0.22, 0.18)
    return jnp.clip(spiked(entries, jax.random.fold_in(key, 3), *heavy), -most, most).astype(dtype)


def setup_inputs(seed: int = 0) -> dict:
    seeds = jax.random.split(jax.random.key(seed), 19)
    return {
        "tokens": gaussian_with(seeds[0], (ROWS, LEN, D), 1.0, 6.0, ((0, 8), (1, 4)), (0, 2, 8, 2.0)),
        "fragments": draw_fragments(jax.random.fold_in(seeds[18], 71), 0),
        "cotangent": normal_values(seeds[2], (ROWS, LEN, D), 1.0, 6.0, ((0, 8), (1, 4))),
        "query_weight": normal_values(seeds[3], (D, D), D ** -0.5, 0.21875, ((0, 8),)),
        "query_bias": normal_values(seeds[4], (D,), 0.3, 1.75, ((0, 8),)),
        "key_weight": normal_values(seeds[5], (D, D), D ** -0.5, 0.21875, ((0, 8),)),
        "value_weight": normal_values(seeds[6], (D, D), D ** -0.5, 0.21875, ((0, 8),)),
        "value_bias": normal_values(seeds[7], (D,), 0.3, 1.75, ((0, 8),)),
        "out_weight": normal_values(seeds[8], (D, D), (D // 32) ** -0.5, 1.25, ((0, 8),)),
        "out_bias": normal_values(seeds[9], (D,), 0.3, 1.75, ((0, 8),)),
        "first_gain": jnp.clip(1.0 + 0.1 * jax.random.normal(seeds[10], (D,), jnp.float32), 0.5, 1.5).astype(jnp.bfloat16),
        "first_shift": normal_values(seeds[11], (D,), 0.3, 1.75, ((0, 8),)),
        "up_weight": normal_values(seeds[12], (D, FF), D ** -0.5, 0.21875, ((0, 8),)),
        "up_bias": normal_values(seeds[13], (FF,), 0.3, 1.75, ((0, 8),)),
        "down_weight": normal_values(seeds[14], (FF, D), FF ** -0.5, 0.109375, ((0, 8),)),
        "down_bias": normal_values(seeds[15], (D,), 0.3, 1.75, ((0, 8),)),
        "second_gain": jnp.clip(1.0 + 0.1 * jax.random.normal(seeds[16], (D,), jnp.float32), 0.5, 1.5).astype(jnp.bfloat16),
        "second_shift": normal_values(seeds[17], (D,), 0.3, 1.75, ((0, 8),)),
    }


@jax.custom_vjp
def low(v):
    return lax.optimization_barrier(v.astype(jnp.bfloat16)).astype(jnp.float32)

@jax.custom_vjp
def low_back(v):
    return v

def low_keep(v):
    return (low(v), None)

def low_pass(kept, grad):
    return (grad,)

def back_keep(v):
    return (v, None)

def back_low(kept, grad):
    return (low(grad),)
low.defvjp(low_keep, low_pass)
low_back.defvjp(back_keep, back_low)

def project(input_tokens, weight_matrix):
    return jnp.einsum('rld,de->rle', input_tokens, weight_matrix, precision=lax.Precision.HIGHEST)

def layer_norm(input_tokens, gain, shift):
    center = input_tokens - lax.optimization_barrier(jnp.mean(input_tokens, axis=-1, keepdims=True))
    spread = lax.optimization_barrier(jnp.mean(center * center, axis=-1, keepdims=True))
    return center * lax.rsqrt(spread + 1e-12) * gain + shift

def layer(params, input_tokens, segments):
    query_weight, query_bias, key_weight, value_weight, value_bias, out_weight, out_bias, first_gain, first_shift, up_weight, up_bias, down_weight, down_bias, second_gain, second_shift = params
    row_count, seq_len, feat_dim = input_tokens.shape
    queries = low_back(low(project(input_tokens, query_weight) + query_bias))
    keys = low_back(low(project(input_tokens, key_weight)))
    values = low_back(low(project(input_tokens, value_weight) + value_bias))
    query_heads = queries.reshape(row_count, seq_len, H, DH)
    key_heads = keys.reshape(row_count, seq_len, H, DH)
    value_heads = values.reshape(row_count, seq_len, H, DH)
    scores = jnp.einsum('bqhd,bkhd->bhqk', query_heads, key_heads, precision=lax.Precision.HIGHEST) * DH ** (-0.5)
    scores = low_back(scores)
    allowed = (segments[:, :, None] == segments[:, None, :])[:, None]
    scores = jnp.where(allowed, scores, -1e+30)
    probs = low(jax.nn.softmax(scores, axis=-1))
    attended = jnp.einsum('bhqk,bkhd->bqhd', probs, value_heads, precision=lax.Precision.HIGHEST)
    attended = low_back(low(attended.reshape(row_count, seq_len, feat_dim)))
    branch = low_back(project(attended, out_weight) + out_bias)
    hidden = layer_norm(input_tokens + branch, first_gain, first_shift)
    before = low_back(project(low(hidden), up_weight) + up_bias)
    active = low(jax.nn.gelu(before, approximate=False))
    second = low_back(project(active, down_weight) + down_bias)
    return layer_norm(hidden + second, second_gain, second_shift)

def reference(tokens, fragments, cotangent, query_weight, query_bias, key_weight, value_weight, value_bias, out_weight, out_bias, first_gain, first_shift, up_weight, up_bias, down_weight, down_bias, second_gain, second_shift):
    params = tuple((item.astype(jnp.float32) for item in (query_weight, query_bias, key_weight, value_weight, value_bias, out_weight, out_bias, first_gain, first_shift, up_weight, up_bias, down_weight, down_bias, second_gain, second_shift)))
    group_rows = math.gcd(ROWS, max(1, 4096 // LEN))
    group_count = ROWS // group_rows
    input_tokens = tokens.astype(jnp.float32).reshape(group_count, group_rows, LEN, D)
    segments = fragments.astype(jnp.int32).reshape(group_count, group_rows, LEN)
    grads_out = cotangent.astype(jnp.float32).reshape(group_count, group_rows, LEN, D)

    def one_group(totals, packed):
        block_in, block_seg, block_cot = packed
        result, pullback = jax.vjp(lambda weights, acts: layer(weights, acts, block_seg), params, block_in)
        grad_params, grad_in = pullback(block_cot)
        totals = tuple((left + right for left, right in zip(totals, grad_params)))
        return (totals, (result.astype(jnp.bfloat16), grad_in.astype(jnp.bfloat16)))
    zeros = tuple((jnp.zeros(item.shape, jnp.float32) for item in params))
    totals, (results, grad_inputs) = lax.scan(one_group, zeros, (input_tokens, segments, grads_out))
    return (results.reshape(ROWS, LEN, D), grad_inputs.reshape(ROWS, LEN, D), totals[0], totals[1], totals[2], totals[3], totals[4], totals[5], totals[6], totals[7], totals[8], totals[9], totals[10], totals[11], totals[12], totals[13], totals[14])
```

```python
import jax
import jax.numpy as jnp
from jax import lax
from jax.sharding import PartitionSpec as P

H = 12
DH = 64

EPS = 1e-12
NEG = -1e30
ROOT_HALF = 0.7071067811865476
DENSITY = 0.3989422804014327
BF = jnp.bfloat16
F32 = jnp.float32


def matmul(a, b):
    return lax.dot_general(a, b, (((1,), (0,)), ((), ())), preferred_element_type=F32)


def matmul_back(a, b):
    return lax.dot_general(a, b, (((1,), (1,)), ((), ())), preferred_element_type=F32)


def outer_sum(a, b):
    return lax.dot_general(a, b, (((0,), (0,)), ((), ())), preferred_element_type=F32)


def total(a):
    return jnp.sum(a.astype(F32), axis=0)


def normalize(rows):
    center = rows - jnp.mean(rows, axis=-1, keepdims=True)
    inverse = lax.rsqrt(jnp.mean(center * center, axis=-1, keepdims=True) + EPS)
    return center * inverse, inverse


def normalize_back(grad, normed, inverse):
    return inverse * (
        grad
        - jnp.mean(grad, axis=-1, keepdims=True)
        - normed * jnp.mean(grad * normed, axis=-1, keepdims=True)
    )


class Links:
    def __init__(self):
        self.nd = lax.axis_size("dp")
        self.nb = lax.axis_size("blk")
        self.bits = self.nb.bit_length() - 1
        self.blk = lax.axis_index("blk")
        self.dp = lax.axis_index("dp")
        n = self.nd
        self.order = list(range(0, n, 2)) + list(range(n - 1, 0, -2))
        place = {d: i for i, d in enumerate(self.order)}
        self.core = self.blk & 1
        self.sign = 1 - 2 * self.core
        self.place = jnp.where(
            self.dp % 2 == 0, self.dp // 2, n - 1 - self.dp // 2
        )
        pairs = []
        for d in range(n):
            for b in range(self.nb):
                step = 1 if b % 2 == 0 else -1
                target = self.order[(place[d] + step) % n]
                pairs.append((d * self.nb + b, target * self.nb + b))
        self.pairs = pairs

    def swap(self, a, bit):
        return lax.ppermute(a, "blk", [(i, i ^ (1 << bit)) for i in range(self.nb)])

    def step(self, a):
        return lax.ppermute(a, ("dp", "blk"), self.pairs)

    def shard_at(self, offset):
        n = self.nd
        at = (self.place + offset) % n
        return jnp.where(at < n // 2, 2 * at, 2 * (n - 1 - at) + 1)

    def to_rows(self, a):
        for bit in reversed(range(self.bits)):
            half = a.shape[0] // 2
            mine = (self.blk >> bit) & 1
            keep = lax.dynamic_slice_in_dim(a, mine * half, half, 0)
            send = lax.dynamic_slice_in_dim(a, (1 - mine) * half, half, 0)
            a = jnp.concatenate([keep, self.swap(send, bit)], axis=1)
        return a

    def from_rows(self, a):
        for bit in range(self.bits):
            half = a.shape[1] // 2
            mine = (self.blk >> bit) & 1
            keep, got = a[:, :half], self.swap(a[:, half:], bit)
            a = jnp.where(
                mine == 0,
                jnp.concatenate([keep, got], 0),
                jnp.concatenate([got, keep], 0),
            )
        return a

    def gather(self, piece):
        n, m = self.nd, piece.shape[0]
        held, now = [], piece
        for _ in range(n // 2 - 1):
            now = self.step(now)
            held.append(now)
        far = self.step(lax.dynamic_slice_in_dim(now, self.core * (m // 2), m // 2, 0))
        packed = jnp.concatenate(held + [far], 0)
        other = self.swap(packed, 0)
        whole = jnp.zeros((n,) + piece.shape, piece.dtype)
        put = lambda w, a, at: lax.dynamic_update_slice(
            w, a[None], (at,) + (0,) * a.ndim
        )
        whole = put(whole, piece, self.dp)
        for s in range(1, n // 2):
            whole = put(whole, packed[(s - 1) * m : s * m], self.shard_at(-self.sign * s))
            whole = put(whole, other[(s - 1) * m : s * m], self.shard_at(self.sign * s))
        tops = jnp.where(self.core == 0, packed[-(m // 2) :], other[-(m // 2) :])
        lows = jnp.where(self.core == 0, other[-(m // 2) :], packed[-(m // 2) :])
        return put(whole, jnp.concatenate([tops, lows], 0), self.shard_at(n // 2))

    def scatter(self, parts):
        n, m = self.nd, parts.shape[1]
        parts = parts.astype(BF)
        pick = lambda at: lax.dynamic_index_in_dim(parts, at, 0, keepdims=False)
        halved = lambda a, c: lax.dynamic_slice_in_dim(a, c * (m // 2), m // 2, 0)
        far = pick(self.shard_at(n // 2))
        send = [pick(self.shard_at(-self.sign * s)) for s in range(1, n // 2)]
        send.append(halved(far, 1 - self.core))
        got = self.swap(jnp.concatenate(send, 0), 0).astype(F32)
        acc = halved(far, self.core).astype(F32) + got[-(m // 2) :]
        moved = self.step(acc.astype(BF)).astype(F32)
        zero = jnp.zeros((m // 2,) + moved.shape[1:], F32)
        moved = jnp.where(
            self.core == 0,
            jnp.concatenate([moved, zero], 0),
            jnp.concatenate([zero, moved], 0),
        )
        for s in range(n // 2 - 1, 0, -1):
            acc = pick(self.shard_at(self.sign * s)).astype(F32) + got[(s - 1) * m : s * m] + moved
            moved = self.step(acc.astype(BF)).astype(F32)
        acc = pick(self.dp).astype(F32) + moved
        for bit in range(self.bits):
            low = acc.astype(BF)
            acc = low.astype(F32) + self.swap(low, bit).astype(F32)
        return acc


def local(
    tokens,
    fragments,
    cotangent,
    query_weight,
    query_bias,
    key_weight,
    value_weight,
    value_bias,
    out_weight,
    out_bias,
    first_gain,
    first_shift,
    up_weight,
    up_bias,
    down_weight,
    down_bias,
    second_gain,
    second_shift,
):
    links = Links()
    n = links.nd
    shard, dim = query_weight.shape
    wide = up_bias.shape[0]
    vectors = (
        query_bias,
        value_bias,
        out_bias,
        first_gain,
        first_shift,
        down_bias,
        second_gain,
        second_shift,
        up_bias,
    )
    count = sum(v.shape[0] for v in vectors)
    used = 3 * shard + -(-count // dim)
    rows = -(-used // 32) * 32

    def pack(q, k, v, vecs, dtype):
        flat = jnp.concatenate([x.astype(dtype) for x in vecs], -1)
        room = (rows - 3 * shard) * dim - count
        flat = jnp.pad(flat, [(0, 0)] * (flat.ndim - 1) + [(0, room)])
        flat = flat.reshape(flat.shape[:-1] + (rows - 3 * shard, dim))
        return jnp.concatenate([q.astype(dtype), k.astype(dtype), v.astype(dtype), flat], -2)

    def unpack(a):
        q, k, v = (a[..., i * shard : (i + 1) * shard, :] for i in range(3))
        flat = a[..., 3 * shard :, :].reshape(a.shape[:-2] + (-1,))
        out, at = [], 0
        for x in vectors:
            out.append(flat[..., at : at + x.shape[0]])
            at += x.shape[0]
        return q, k, v, out

    first = links.gather(pack(query_weight, key_weight, value_weight, vectors, BF))
    ids = links.to_rows(fragments)
    x = links.to_rows(tokens)
    count_rows, length = ids.shape
    second_group = links.gather(jnp.concatenate([out_weight, up_weight], 1))
    third = links.gather(down_weight)
    g = links.to_rows(cotangent)

    q_w, k_w, v_w, vecs = unpack(first)
    q_w, k_w, v_w = (w.reshape(dim, dim) for w in (q_w, k_w, v_w))
    q_b, v_b, o_b, gain1, shift1, d_b, gain2, shift2, u_b = (
        v.reshape(-1).astype(F32) for v in vecs
    )
    second_group = second_group.reshape(dim, dim + wide * n)
    o_w, u_w = second_group[:, :dim], second_group[:, dim:]
    d_w = third.reshape(-1, dim)

    x = x.reshape(-1, dim)
    g = g.reshape(-1, dim).astype(F32)
    heads = lambda a: a.reshape(count_rows, length, H, DH).transpose(0, 2, 1, 3)
    merge = lambda a: a.transpose(0, 2, 1, 3).reshape(-1, dim)
    factor = DH**-0.5
    q = (matmul(x, q_w) + q_b).astype(BF)
    k = matmul(x, k_w).astype(BF)
    v = (matmul(x, v_w) + v_b).astype(BF)
    qh, kh, vh = heads(q), heads(k), heads(v)
    allowed = (ids[:, :, None] == ids[:, None, :])[:, None]
    scores = jnp.einsum("rhqd,rhkd->rhqk", qh, kh, preferred_element_type=F32) * factor
    scores = jnp.where(allowed, scores, NEG)
    top = jnp.max(scores, axis=-1, keepdims=True)
    e = jnp.exp(scores - top)
    probs = e / jnp.sum(e, axis=-1, keepdims=True)
    low = probs.astype(BF)
    full = jnp.einsum("rhqk,rhkd->rhqd", low, vh, preferred_element_type=F32)
    attended = merge(full.astype(BF))
    r1 = x.astype(F32) + matmul(attended, o_w) + o_b
    n1, i1 = normalize(r1)
    hidden = n1 * gain1 + shift1
    hidden_low = hidden.astype(BF)
    before = matmul(hidden_low, u_w) + u_b
    phi = 0.5 * (1.0 + lax.erf(before * ROOT_HALF))
    active = (before * phi).astype(BF)
    slope = phi + before * DENSITY * jnp.exp(-0.5 * before * before)
    n2, i2 = normalize(hidden + matmul(active, d_w) + d_b)
    result = (n2 * gain2 + shift2).astype(BF)
    result = links.from_rows(result.reshape(count_rows, length, dim))

    grad_shift2 = total(g)
    grad_gain2 = total(g * n2)
    g_r2 = normalize_back(g * gain2, n2, i2)
    g_second = g_r2.astype(BF)
    grad_down_bias = total(g_second)
    grad_down = outer_sum(active, g_second)
    grad_down = links.scatter(grad_down.reshape(n, -1, dim))
    g_before = (matmul_back(g_second, d_w) * slope).astype(BF)
    grad_up_bias = total(g_before)
    grad_up = outer_sum(hidden_low, g_before)
    g_hidden = g_r2 + matmul_back(g_before, u_w)
    grad_shift1 = total(g_hidden)
    grad_gain1 = total(g_hidden * n1)
    g_r1 = normalize_back(g_hidden * gain1, n1, i1)
    g_branch = g_r1.astype(BF)
    grad_out_bias = total(g_branch)
    grad_out = outer_sum(attended, g_branch)
    both = links.scatter(
        jnp.concatenate([grad_out, grad_up], 1).reshape(n, shard, -1)
    )
    grad_out, grad_up = both[:, :dim], both[:, dim:]
    gh = heads(matmul_back(g_branch, o_w).astype(BF))
    g_v = jnp.einsum("rhqk,rhqd->rhkd", low, gh, preferred_element_type=F32)
    g_p = jnp.einsum("rhqd,rhkd->rhqk", gh, vh, preferred_element_type=F32)
    delta = jnp.sum(probs * g_p, axis=-1, keepdims=True)
    g_s = (probs * (g_p - delta)).astype(BF)
    g_q = jnp.einsum("rhqk,rhkd->rhqd", g_s, kh, preferred_element_type=F32) * factor
    g_k = jnp.einsum("rhqk,rhqd->rhkd", g_s, qh, preferred_element_type=F32) * factor
    g_q, g_k, g_v = (merge(a.astype(BF)) for a in (g_q, g_k, g_v))
    g_x = g_r1 + matmul_back(g_q, q_w) + matmul_back(g_k, k_w) + matmul_back(g_v, v_w)
    g_x = links.from_rows(g_x.astype(BF).reshape(count_rows, length, dim))
    sums = (
        total(g_q),
        total(g_v),
        grad_out_bias,
        grad_gain1,
        grad_shift1,
        grad_down_bias,
        grad_gain2,
        grad_shift2,
        grad_up_bias,
    )
    weights = (outer_sum(x, a).reshape(n, shard, dim) for a in (g_q, g_k, g_v))
    last = links.scatter(pack(*weights, tuple(s.reshape(n, -1) for s in sums), BF))
    grad_q, grad_k, grad_v, vecs = unpack(last)
    (
        grad_q_b,
        grad_v_b,
        grad_out_bias,
        grad_gain1,
        grad_shift1,
        grad_down_bias,
        grad_gain2,
        grad_shift2,
        grad_up_bias,
    ) = vecs
    return (
        result,
        g_x,
        grad_q,
        grad_q_b,
        grad_k,
        grad_v,
        grad_v_b,
        grad_out,
        grad_out_bias,
        grad_gain1,
        grad_shift1,
        grad_up,
        grad_up_bias,
        grad_down,
        grad_down_bias,
        grad_gain2,
        grad_shift2,
    )


def solution(mesh):
    three, two, one = P("dp", "blk", None), P("dp", None), P("dp")
    params = (two, one, two, two, one, two, one, one, one, two, one, two, one, one, one)
    return jax.shard_map(
        local,
        mesh=mesh,
        in_specs=(three, P("dp", "blk"), three) + params,
        out_specs=(three, three) + params,
        check_vma=False,
    )
```

```python
import functools

import jax
import jax.numpy as jnp
from jax import lax
from jax.experimental import pallas as pl
from jax.experimental.pallas import tpu as pltpu
from jax.sharding import PartitionSpec as P

H = 12
DH = 64
VECTOR_ROWS = 32
SUM_ROWS = 32
TILE = 256
QUERIES = 256

EPS = 1e-12
NEG = -1e30
ROOT_HALF = 0.7071067811865476
DENSITY = 0.3989422804014327
BF = jnp.bfloat16
F32 = jnp.float32
MIB = 1 << 20

QB, VB, OB, G1, S1, DB, G2, S2, UB = range(9)


def dot(a, b, left, right):
    return lax.dot_general(a, b, (((left,), (right,)), ((), ())), preferred_element_type=F32)


def normalize(rows):
    center = rows - jnp.mean(rows, axis=-1, keepdims=True)
    inverse = lax.rsqrt(jnp.mean(center * center, axis=-1, keepdims=True) + EPS)
    return center * inverse, inverse


def normalize_back(grad, normed, inverse):
    return inverse * (
        grad
        - jnp.mean(grad, axis=-1, keepdims=True)
        - normed * jnp.mean(grad * normed, axis=-1, keepdims=True)
    )


def total(a):
    return jnp.sum(a, axis=0, keepdims=True)


def params(limit=56):
    return pltpu.CompilerParams(vmem_limit_bytes=limit * MIB)


def cost(flops, moved, extra=0):
    return pl.CostEstimate(flops=int(flops), bytes_accessed=int(moved), transcendentals=int(extra))


def flat(ref, columns=slice(None)):
    a = ref[:, :, columns]
    return a.reshape(a.shape[0] * a.shape[1], a.shape[2])


def held(shape):
    return pl.BlockSpec(shape, lambda *_: (0,) * len(shape), pipeline_mode=pl.Buffered(1))


HELD = pl.BlockSpec(memory_space=pl.ANY)
SCALARS = pl.BlockSpec(memory_space=pltpu.SMEM)


def tiled(width, tile=TILE):
    return pl.BlockSpec((tile, width), lambda i: (i, 0))


def fixed(shape):
    return pl.BlockSpec(shape, lambda *_: (0,) * len(shape))


class Links:
    def __init__(self):
        self.nd = lax.axis_size("dp")
        self.nb = lax.axis_size("blk")
        self.bits = self.nb.bit_length() - 1
        self.blk = lax.axis_index("blk")
        self.dp = lax.axis_index("dp")
        n = self.nd
        self.order = list(range(0, n, 2)) + list(range(n - 1, 0, -2))
        place = {d: i for i, d in enumerate(self.order)}
        self.core = self.blk & 1
        self.sign = 1 - 2 * self.core
        self.place = jnp.where(self.dp % 2 == 0, self.dp // 2, n - 1 - self.dp // 2)
        pairs = []
        for d in range(n):
            for b in range(self.nb):
                step = 1 if b % 2 == 0 else -1
                target = self.order[(place[d] + step) % n]
                pairs.append((d * self.nb + b, target * self.nb + b))
        self.pairs = pairs
        far = n // 2
        at = [self.dp]
        at += [self.shard_at(-self.sign * s) for s in range(1, far)]
        at += [self.shard_at(self.sign * s) for s in range(1, far)]
        at += [self.shard_at(far), self.core]
        self.sources = jnp.stack(at).astype(jnp.int32)
        at = [self.shard_at(-self.sign * s) for s in range(1, far)]
        at += [self.shard_at(far)]
        at += [self.shard_at(self.sign * s) for s in range(1, far)]
        at += [self.dp]
        self.targets = jnp.stack(at).astype(jnp.int32)

    def swap(self, a, bit):
        return lax.ppermute(a, "blk", [(i, i ^ (1 << bit)) for i in range(self.nb)])

    def step(self, a):
        return lax.ppermute(a, ("dp", "blk"), self.pairs)

    def shard_at(self, offset):
        n = self.nd
        at = (self.place + offset) % n
        return jnp.where(at < n // 2, 2 * at, 2 * (n - 1 - at) + 1)

    def to_rows(self, a):
        for bit in reversed(range(self.bits)):
            half = a.shape[0] // 2
            mine = (self.blk >> bit) & 1
            keep = lax.dynamic_slice_in_dim(a, mine * half, half, 0)
            send = lax.dynamic_slice_in_dim(a, (1 - mine) * half, half, 0)
            got = self.swap(send, bit)
            yield got
            a = jnp.concatenate([keep, got], axis=1)
        yield a

    def from_rows(self, a):
        for bit in range(self.bits):
            half = a.shape[1] // 2
            mine = (self.blk >> bit) & 1
            keep, got = a[:, :half], self.swap(a[:, half:], bit)
            yield got
            a = jnp.where(
                mine == 0,
                jnp.concatenate([keep, got], 0),
                jnp.concatenate([got, keep], 0),
            )
        yield a

    def gather(self, piece, waits=()):
        n, m = self.nd, piece.shape[0]
        mine, other, now = [], [], piece
        waits = dict(enumerate(waits))
        for i in range(n // 2 - 1):
            if i in waits:
                now = after(now, waits[i])
            now = self.step(now)
            mine.append(now)
            other.append(self.swap(now, 0))
        far = self.step(lax.dynamic_slice_in_dim(now, self.core * (m // 2), m // 2, 0))
        return [piece] + mine + other + [far, self.swap(far, 0)]

    def whole(self, pieces):
        n = self.nd
        out = jnp.zeros((n,) + pieces[0].shape, pieces[0].dtype)
        for i, a in enumerate(pieces[:-2]):
            out = lax.dynamic_update_slice(out, a[None], (self.sources[i], 0, 0))
        a, b = pieces[-2:]
        far = jnp.where(self.core == 0, jnp.concatenate([a, b], 0), jnp.concatenate([b, a], 0))
        return lax.dynamic_update_slice(out, far[None], (self.sources[n - 1], 0, 0))

    def split(self, parts):
        pick = lambda i: lax.dynamic_index_in_dim(parts, self.targets[i], 0, keepdims=False)
        half = self.nd // 2
        return (
            jnp.stack([pick(i) for i in range(half)]),
            jnp.stack([pick(i) for i in range(half - 1, self.nd)]),
        )

    def scatter(self, send, keep):
        n, m = self.nd, keep.shape[1]
        far = n // 2
        got = self.swap(send, 0)
        yield got
        halved = lambda a: lax.dynamic_slice_in_dim(a, self.core * (m // 2), m // 2, 0).astype(F32)
        acc = halved(keep[0]) + halved(got[far - 1])
        moved = self.step(acc.astype(BF))
        yield moved
        zero = jnp.zeros((m // 2,) + moved.shape[1:], BF)
        moved = jnp.where(
            self.core == 0,
            jnp.concatenate([moved, zero], 0),
            jnp.concatenate([zero, moved], 0),
        )
        for s in range(far - 1, 0, -1):
            acc = keep[s].astype(F32) + got[s - 1].astype(F32) + moved.astype(F32)
            moved = self.step(acc.astype(BF))
            yield moved
        acc = keep[far].astype(F32) + moved.astype(F32)
        for bit in range(self.bits):
            low = acc.astype(BF)
            moved = self.swap(low, bit)
            yield moved
            acc = low.astype(F32) + moved.astype(F32)
        yield acc


class Group:
    def __init__(self, arrays, parts, pieces, width):
        self.arrays, self.parts, self.pieces, self.width = arrays, parts, pieces, width
        self.n_refs = len(arrays)
        self.specs = [held(a.shape) for a in arrays]

    def scratch(self, names, n):
        shape = lambda rows: (n, rows) if self.pieces else (1, n * rows)
        return [
            pltpu.VMEM(shape(rows) + (self.width,), BF) for rows, name in self.parts if name in names
        ]

    def fetch(self, refs, sources, names, into):
        into = dict(zip(names, into))
        if not self.pieces:
            for (_, name), ref in zip(self.parts, refs):
                if name in names:
                    into[name][0] = ref[...]
            return
        n = self.n_refs - 1
        half = sum(rows for rows, _ in self.parts) // 2
        starts = [sum(rows for rows, _ in self.parts[:i]) for i in range(len(self.parts))]
        for i in range(n - 1):
            for start, (rows, name) in zip(starts, self.parts):
                if name in names:
                    into[name][sources[i]] = refs[i][start : start + rows]
        for core in range(2):

            @pl.when(sources[n] == core)
            def _(core=core):
                for start, (rows, name) in zip(starts, self.parts):
                    for h in range(2):
                        low, high = max(start, h * half), min(start + rows, (h + 1) * half)
                        if name in names and low < high:
                            ref = refs[n - 1] if h == core else refs[n]
                            into[name][sources[n - 1], low - start : high - start] = ref[
                                low - h * half : high - h * half
                            ]


def pack(weights, vectors):
    shard, dim = weights[0].shape

    def kernel(*refs):
        mats, vecs, out_ref, table = refs[: len(weights)], refs[len(weights) : -2], refs[-2], refs[-1]
        for i, ref in enumerate(mats):
            out_ref[i * shard : (i + 1) * shard] = ref[...]
        table[...] = jnp.zeros_like(table)
        line = 0
        for ref in vecs:
            a = ref[...].astype(F32)
            for t in range(a.shape[0] // shard):
                table[line : line + 1, :shard] = a[t * shard : (t + 1) * shard].reshape(1, shard)
                line += 1
        blank = jnp.zeros((VECTOR_ROWS, dim - 128), F32)
        out_ref[len(mats) * shard :] = jnp.concatenate([table[...], blank], 1).astype(BF)

    return pl.pallas_call(
        kernel,
        out_shape=jax.ShapeDtypeStruct((len(weights) * shard + VECTOR_ROWS, dim), BF),
        scratch_shapes=[pltpu.VMEM((VECTOR_ROWS, 128), F32)],
        compiler_params=params(),
        cost_estimate=cost(0, 4 * len(weights) * shard * dim),
        name="pack",
    )(*weights, *vectors)


def after(a, *others):
    return lax.optimization_barrier((a,) + others)[0]


def lay(links, group, names, spread=None):
    n = links.nd
    k = group.n_refs
    sizes = {name: rows for rows, name in group.parts}
    tables = 0 if spread is None else 1

    def kernel(*refs):
        sources, pieces = refs[0], refs[1 : 1 + k]
        outs = refs[1 + k + tables :]
        group.fetch(pieces, sources, names, outs)
        if tables:
            lines = outs[-2][...].astype(F32).reshape(n, VECTOR_ROWS, group.width)[:, :, :128]
            wide = jnp.concatenate([lines[j] for j in range(n)], 1).astype(BF)
            outs[-1][...] = dot(wide, refs[1 + k][...], 1, 0)

    shapes = [((n, sizes[x]) if group.pieces else (1, n * sizes[x])) + (group.width,) for x in names]
    out_shape = [jax.ShapeDtypeStruct(x, BF) for x in shapes]
    args = [links.sources, *group.arrays]
    specs = [SCALARS] + group.specs
    if tables:
        args.append(spread)
        specs.append(held(spread.shape))
        out_shape.append(jax.ShapeDtypeStruct((VECTOR_ROWS, group.width), F32))
    out = pl.pallas_call(
        kernel,
        grid=(1,),
        in_specs=specs,
        out_specs=[held(x.shape) for x in out_shape],
        out_shape=out_shape,
        compiler_params=params(),
        cost_estimate=cost(0, sum(4 * x.size for x in out_shape)),
        name="lay",
    )(*args)
    return [x.reshape(-1, group.width) for x in out]


def head_masks(width):
    lane = lax.broadcasted_iota(jnp.int32, (1, width), 1)
    return [lane // DH == h for h in range(width // DH)]


def fill_bias(bias, down_ref, across_ref):
    bias[...] = jnp.where(down_ref[...][:, :1] == across_ref[0], 0.0, NEG)


def attend(q, k, v, down, across):
    rows, _, length = across.shape
    dim = q.shape[1]
    pairs = dim // 128

    def kernel(down_ref, across_ref, q_ref, k_ref, v_ref, o_ref, log_ref, bias):
        @pl.when(pl.program_id(1) == 0)
        def _():
            fill_bias(bias, down_ref, across_ref)

        masks = head_masks(128)
        keys, values_t = k_ref[...], v_ref[...].astype(F32).T.astype(BF)
        scaled = q_ref[...].astype(F32) * DH**-0.5
        for at in range(0, length, QUERIES):
            span = slice(at, at + QUERIES)
            outs = []
            for h, mask in enumerate(masks):
                one = jnp.where(mask, scaled[span], 0.0).astype(BF)
                s = dot(keys, one, 1, 1) + bias[:, span]
                top = jnp.max(s, axis=0, keepdims=True)
                e = jnp.exp(s - top)
                sums = jnp.sum(e, axis=0, keepdims=True)
                o = dot(values_t[h * DH : (h + 1) * DH], e.astype(BF), 1, 0)
                outs.append(o / sums)
                log_ref[0, 0, h : h + 1, span] = top + jnp.log(sums)
            o_ref[span] = jnp.concatenate(outs, 0).T.astype(BF)

    block = pl.BlockSpec((length, 128), lambda r, h: (r, h))
    return pl.pallas_call(
        kernel,
        grid=(rows, pairs),
        in_specs=[
            pl.BlockSpec((length, 128), lambda r, h: (r, 0)),
            pl.BlockSpec((1, 1, length), lambda r, h: (r, 0, 0)),
            block,
            block,
            block,
        ],
        out_specs=[block, pl.BlockSpec((1, 1, 2, length), lambda r, h: (r, h, 0, 0))],
        out_shape=[
            jax.ShapeDtypeStruct(q.shape, BF),
            jax.ShapeDtypeStruct((rows, pairs, 2, length), F32),
        ],
        scratch_shapes=[pltpu.VMEM((length, length), F32)],
        compiler_params=params(),
        cost_estimate=cost(
            16 * rows * H * length * length * DH, 8 * rows * length * dim, rows * H * length * length
        ),
        name="attend",
    )(down, across, q, k, v)


def attend_back(q, k, v, g, logs, down, across, row, grads):
    rows, _, length = across.shape
    dim = q.shape[1]
    pairs = dim // 128

    grads = grads or ()

    def kernel(down_ref, across_ref, q_ref, k_ref, v_ref, g_ref, log_ref, *refs):
        gq_ref, gk_ref, gv_ref, bias = refs[len(grads) :]

        @pl.when(pl.program_id(0) == 0)
        def _():
            fill_bias(bias, down_ref, across_ref)

        masks = head_masks(128)
        keys, values, keys_t = k_ref[...], v_ref[...], k_ref[...].astype(F32).T.astype(BF)
        scaled = q_ref[...].astype(F32) * DH**-0.5
        grad = g_ref[...].astype(F32)
        scaled_low = scaled.astype(BF)
        gk = [0.0] * len(masks)
        gv = [0.0] * len(masks)
        for at in range(0, length, QUERIES):
            span = slice(at, at + QUERIES)
            outs = []
            for h, mask in enumerate(masks):
                one = jnp.where(mask, scaled[span], 0.0).astype(BF)
                s = dot(keys, one, 1, 1) + bias[:, span]
                p = jnp.exp(s - log_ref[0, 0, h : h + 1, span])
                one_g = jnp.where(mask, grad[span], 0.0).astype(BF)
                t = p * dot(values, one_g, 1, 1)
                gs = (t - p * jnp.sum(t, axis=0, keepdims=True)).astype(BF)
                gv[h] += dot(p.astype(BF), g_ref[span], 1, 0)
                gk[h] += dot(gs, scaled_low[span], 1, 0)
                outs.append(dot(keys_t[h * DH : (h + 1) * DH], gs, 1, 0))
            gq_ref[span] = (jnp.concatenate(outs, 0).T * DH**-0.5).astype(BF)
        gk_ref[...] = jnp.where(masks[0], gk[0], gk[1]).astype(BF)
        gv_ref[...] = jnp.where(masks[0], gv[0], gv[1]).astype(BF)

    block = pl.BlockSpec((length, 128), lambda h: (row, h))
    out = jax.ShapeDtypeStruct(q.shape, BF)
    return pl.pallas_call(
        kernel,
        grid=(pairs,),
        in_specs=[
            pl.BlockSpec((length, 128), lambda h: (row, 0)),
            pl.BlockSpec((1, 1, length), lambda h: (row, 0, 0)),
            block,
            block,
            block,
            block,
            pl.BlockSpec((1, 1, 2, length), lambda h: (row, h, 0, 0)),
        ]
        + [HELD] * len(grads),
        out_specs=[block] * 3,
        out_shape=[out] * 3,
        input_output_aliases={7 + i: i for i in range(len(grads))},
        scratch_shapes=[pltpu.VMEM((length, length), F32)],
        compiler_params=params(),
        cost_estimate=cost(
            40 * H * length * length * DH, 14 * length * dim, H * length * length
        ),
        name="attend_back",
    )(down, across, q, k, v, g, logs, *grads)


def halves(n, rows, width):
    return [
        jax.ShapeDtypeStruct((n // 2, rows, width), BF),
        jax.ShapeDtypeStruct((n // 2 + 1, rows, width), BF),
    ]


def outer_rows(links, a, b):
    tokens, wide = a.shape
    dim = b.shape[1]
    n = links.nd
    rows = wide // n
    far = n // 2

    def kernel(targets, a_ref, b_ref, send_ref, keep_ref):
        i = pl.program_id(0)
        low = dot(a_ref[...], b_ref[...], 0, 0).astype(BF)

        @pl.when(i < far)
        def _():
            send_ref[0] = low

        @pl.when(i >= far - 1)
        def _():
            keep_ref[0] = low

    return pl.pallas_call(
        kernel,
        grid_spec=pltpu.PrefetchScalarGridSpec(
            num_scalar_prefetch=1,
            grid=(n,),
            in_specs=[
                pl.BlockSpec((tokens, rows), lambda i, at: (0, at[i])),
                pl.BlockSpec((tokens, dim), lambda i, at: (0, 0)),
            ],
            out_specs=[
                pl.BlockSpec((1, rows, dim), lambda i, at: (jnp.minimum(i, far - 1), 0, 0)),
                pl.BlockSpec((1, rows, dim), lambda i, at: (jnp.maximum(i - far + 1, 0), 0, 0)),
            ],
        ),
        out_shape=halves(n, rows, dim),
        compiler_params=params(),
        cost_estimate=cost(2 * tokens * dim * wide, 2 * (tokens + dim) * wide),
        name="outer_rows",
    )(links.targets, a, b)


def store_shards(targets, rows, block, value, send_ref, keep_ref, start):
    n = targets.shape[0]
    far = n // 2
    block[...] = value.astype(BF).reshape(block.shape)
    for i in range(n):
        piece = block[targets[i]]
        if i < far:
            send_ref[i, pl.ds(start, rows), :] = piece
        if i >= far - 1:
            keep_ref[i - far + 1, pl.ds(start, rows), :] = piece


def outer_columns(links, pairs):
    tokens, dim = pairs[0][0].shape
    n = links.nd
    rows = dim // n
    far = n // 2
    (a0, b0), (a1, b1) = pairs
    steps = b1.shape[1] // dim + 1

    def kernel(targets, a0_ref, b0_ref, a1_ref, b1_ref, send_ref, keep_ref, block):
        i = pl.program_id(0)

        @pl.when(i == 0)
        def _():
            value = dot(a0_ref[...], b0_ref[...], 0, 0)
            store_shards(targets, rows, block, value, send_ref, keep_ref, 0)

        @pl.when(i > 0)
        def _():
            value = dot(a1_ref[...], b1_ref[...], 0, 0)
            store_shards(targets, rows, block, value, send_ref, keep_ref, 0)

    whole = pl.BlockSpec((tokens, dim), lambda i: (0, 0))
    width = dim * steps
    return pl.pallas_call(
        kernel,
        grid=(steps,),
        in_specs=[
            SCALARS,
            whole,
            whole,
            whole,
            pl.BlockSpec((tokens, dim), lambda i: (0, jnp.maximum(i - 1, 0))),
        ],
        out_specs=[
            pl.BlockSpec((far, rows, dim), lambda i: (0, 0, i)),
            pl.BlockSpec((far + 1, rows, dim), lambda i: (0, 0, i)),
        ],
        out_shape=halves(n, rows, width),
        scratch_shapes=[pltpu.VMEM((n, rows, dim), BF)],
        compiler_params=params(),
        cost_estimate=cost(2 * tokens * dim * width, 2 * (tokens + dim) * width),
        name="outer_columns",
    )(links.targets, a0, b0, a1, b1)


def outer_last(links, x, grads, sums, spread):
    tokens, dim = x.shape
    n = links.nd
    rows = dim // n
    far = n // 2
    deep = len(grads) * rows + SUM_ROWS

    def kernel(targets, x_ref, q_ref, k_ref, v_ref, sums_ref, spread_ref, send_ref, keep_ref, block):
        for t, ref in enumerate((q_ref, k_ref, v_ref)):
            store_shards(
                targets, rows, block, dot(x_ref[...], ref[...], 0, 0), send_ref, keep_ref, t * rows
            )
        line = lax.broadcasted_iota(jnp.int32, (SUM_ROWS, 1), 0)
        table = sums_ref[...]
        table = jnp.where(line == QB, total(q_ref[...].astype(F32)), table)
        table = jnp.where(line == VB, total(v_ref[...].astype(F32)), table)
        table = table.astype(BF)
        blank = jnp.zeros((SUM_ROWS, dim - 128), F32)
        start = len(grads) * rows
        for i in range(n):
            part = dot(table, spread_ref[targets[i]], 1, 1)
            part = jnp.concatenate([part, blank], 1).astype(BF)
            if i < far:
                send_ref[i, pl.ds(start, SUM_ROWS), :] = part
            if i >= far - 1:
                keep_ref[i - far + 1, pl.ds(start, SUM_ROWS), :] = part

    whole = fixed((tokens, dim))
    return pl.pallas_call(
        kernel,
        grid=(1,),
        in_specs=[SCALARS] + [whole] * 4 + [fixed(sums.shape), fixed((n, 128, dim))],
        out_specs=[fixed((far, deep, dim)), fixed((far + 1, deep, dim))],
        out_shape=halves(n, deep, dim),
        scratch_shapes=[pltpu.VMEM((n, rows, dim), BF)],
        compiler_params=params(),
        cost_estimate=cost(6 * tokens * dim * dim, 8 * tokens * dim + 6 * dim * dim),
        name="outer_last",
    )(links.targets, x, *grads, sums, spread.reshape(n, 128, dim))


def local(
    tokens,
    fragments,
    cotangent,
    query_weight,
    query_bias,
    key_weight,
    value_weight,
    value_bias,
    out_weight,
    out_bias,
    first_gain,
    first_shift,
    up_weight,
    up_bias,
    down_weight,
    down_bias,
    second_gain,
    second_shift,
):
    links = Links()
    n = links.nd
    shard, dim = query_weight.shape
    times = up_bias.shape[0] // shard
    aligned = shard % 32 == 0

    vectors = [query_bias, value_bias, out_bias, first_gain, first_shift, down_bias, second_gain, second_shift]
    vectors.append(up_bias)
    piece = pack([query_weight, key_weight, value_weight, out_weight], vectors)
    ids_steps = links.to_rows(fragments)
    ids_moved = next(ids_steps)
    x_steps = links.to_rows(after(tokens, ids_moved))
    x_moved = next(x_steps)
    first = links.gather(piece, [piece, ids_moved, x_moved])
    *_, ids = ids_steps
    *_, x = x_steps
    rows, length = ids.shape
    ups = links.gather(up_weight, [first[n // 2 - 1]])
    downs = links.gather(down_weight, [ups[1]])
    *_, g = links.to_rows(after(cotangent, first[-1]))

    parts = [(shard, name) for name in "qkvo"] + [(VECTOR_ROWS, "vec")]
    if not aligned:
        w = links.whole(first)
        first = [w[:, i * shard : (i + 1) * shard].reshape(dim, dim) for i in range(4)]
        first.append(w[:, 4 * shard :].reshape(n * VECTOR_ROWS, dim))
        ups = [links.whole(ups).reshape(dim, -1)]
        downs = [links.whole(downs).reshape(-1, dim)]
    first = Group(first, parts, aligned, dim)
    ups = Group(ups, [(shard, "u")], aligned, times * dim)
    downs = Group(downs, [(times * shard, "d")], aligned, dim)

    at = lax.broadcasted_iota(jnp.int32, (n * 128, dim), 0)
    lane = lax.broadcasted_iota(jnp.int32, (n * 128, dim), 1)
    spread = ((at % 128 < shard) & (lane == at // 128 * shard + at % 128)).astype(BF)

    x = x.reshape(-1, dim)
    g = g.reshape(-1, dim)
    across = ids[:, None, :]
    down = jnp.broadcast_to(ids.reshape(-1, 1), (rows * length, 128))

    q_w, k_w, v_w, o_w, _, table = lay(links, first, ["q", "k", "v", "o", "vec"], spread)
    row = lambda i: table[i : i + 1]
    up_row = table[UB : UB + times].reshape(times, n, shard).transpose(1, 0, 2).reshape(1, -1)
    q = (dot(x, q_w, 1, 0) + row(QB)).astype(BF)
    k = dot(x, k_w, 1, 0).astype(BF)
    v = (dot(x, v_w, 1, 0) + row(VB)).astype(BF)
    heads = lambda a: a.reshape(rows, length, H, DH).transpose(0, 2, 1, 3)
    merge = lambda a: a.transpose(0, 2, 1, 3).reshape(-1, dim)
    qh, kh, vh = heads(q), heads(k), heads(v)
    allowed = (ids[:, :, None] == ids[:, None, :])[:, None]
    scores = jnp.einsum("rhqd,rhkd->rhqk", qh, kh, preferred_element_type=F32) * DH**-0.5
    scores = jnp.where(allowed, scores, NEG)
    e = jnp.exp(scores - jnp.max(scores, axis=-1, keepdims=True))
    probs = e / jnp.sum(e, axis=-1, keepdims=True)
    plow = probs.astype(BF)
    attended = merge(jnp.einsum("rhqk,rhkd->rhqd", plow, vh, preferred_element_type=F32).astype(BF))
    n1, inv1 = normalize(x.astype(F32) + dot(attended, o_w, 1, 0) + row(OB))
    hidden = n1 * row(G1) + row(S1)
    low = hidden.astype(BF)
    (u_w,) = lay(links, ups, ["u"])
    before = dot(low, u_w, 1, 0) + up_row
    phi = 0.5 * (1.0 + lax.erf(before * ROOT_HALF))
    active = (before * phi).astype(BF)
    slope = (phi + before * (DENSITY * jnp.exp(-0.5 * before * before))).astype(BF)
    (d_w,) = lay(links, downs, ["d"])
    n2, inv2 = normalize(hidden + dot(active, d_w, 1, 0) + row(DB))
    result = (n2 * row(G2) + row(S2)).astype(BF)
    grad = g.astype(F32)
    g_r2 = normalize_back(grad * row(G2), n2, inv2)
    g_second = g_r2.astype(BF)
    sums2 = jnp.concatenate([total(g_second.astype(F32)), total(grad * n2), total(grad)], 0)
    if aligned and not dim:
        send, keep = outer_rows(links, active, g_second)
    else:
        send, keep = links.split(dot(active, g_second, 0, 0).astype(BF).reshape(n, -1, dim))
    down_steps = links.scatter(send, keep)
    result_steps = links.from_rows(result.reshape(rows, length, dim))
    g_before = (dot(g_second, d_w, 1, 1) * slope.astype(F32)).astype(BF)
    sums_up = total(g_before.astype(F32))
    g_before = after(g_before, next(down_steps), next(result_steps))
    g_hidden = g_r2 + dot(g_before, u_w, 1, 1)
    g_r1 = normalize_back(g_hidden * row(G1), n1, inv1)
    g_branch = g_r1.astype(BF)
    sums1 = jnp.concatenate([total(g_branch.astype(F32)), total(g_hidden * n1), total(g_hidden)], 0)
    g_att = dot(g_branch, o_w, 1, 1).astype(BF)
    g_branch = after(g_branch, next(down_steps), next(result_steps))
    if aligned and not dim:
        send, keep = outer_columns(links, [(attended, g_branch), (low, g_before)])
    else:
        both = [dot(attended, g_branch, 0, 0), dot(low, g_before, 0, 0)]
        send, keep = links.split(jnp.concatenate(both, 1).astype(BF).reshape(n, shard, -1))
    up_steps = links.scatter(send, keep)
    g_att = after(g_att, next(down_steps), keep)
    g_att = after(g_att, next(down_steps), next(up_steps))
    gh = heads(g_att)
    gv = jnp.einsum("rhqk,rhqd->rhkd", plow, gh, preferred_element_type=F32)
    gp = jnp.einsum("rhqd,rhkd->rhqk", gh, vh, preferred_element_type=F32)
    gs = (probs * (gp - jnp.sum(probs * gp, axis=-1, keepdims=True))).astype(BF)
    gq = jnp.einsum("rhqk,rhkd->rhqd", gs, kh, preferred_element_type=F32) * DH**-0.5
    gk = jnp.einsum("rhqk,rhqd->rhkd", gs, qh, preferred_element_type=F32) * DH**-0.5
    gq, gk, gv = (merge(a.astype(BF)) for a in (gq, gk, gv))
    gq = after(gq, next(down_steps), next(up_steps))
    up_sums = sums_up[0].reshape(n, times, shard).transpose(1, 0, 2).reshape(times, dim)
    zero = jnp.zeros((1, dim), F32)
    sums = jnp.concatenate([zero, zero, sums1, sums2, up_sums], 0)
    sums = jnp.pad(sums, ((0, SUM_ROWS - sums.shape[0]), (0, 0)))
    if aligned and not dim:
        send, keep = outer_last(links, x, (gq, gk, gv), sums, spread)
    else:
        sums = sums.at[QB].set(jnp.sum(gq.astype(F32), 0)).at[VB].set(jnp.sum(gv.astype(F32), 0))
        sums = jnp.pad(
            sums.astype(BF).reshape(SUM_ROWS, n, shard).transpose(1, 0, 2),
            ((0, 0), (0, 0), (0, dim - shard)),
        )
        each = [dot(x, a, 0, 0).astype(BF).reshape(n, shard, dim) for a in (gq, gk, gv)]
        send, keep = links.split(jnp.concatenate(each + [sums], 1))
    last_steps = links.scatter(send, keep)
    gq = after(gq, next(down_steps), next(up_steps), keep)
    g_x = (g_r1 + dot(gq, q_w, 1, 1) + dot(gk, k_w, 1, 1) + dot(gv, v_w, 1, 1)).astype(BF)
    g_x = after(g_x, next(down_steps), next(up_steps), next(last_steps))
    *_, g_x = links.from_rows(g_x.reshape(rows, length, dim))
    *_, result = result_steps
    *_, grad_down = down_steps
    *_, both = up_steps
    *_, last = last_steps
    grad_q, grad_k, grad_v = (last[i * shard : (i + 1) * shard] for i in range(3))
    vecs = last[3 * shard :, :shard]
    return (
        result,
        g_x,
        grad_q,
        vecs[QB],
        grad_k,
        grad_v,
        vecs[VB],
        both[:, :dim],
        vecs[OB],
        vecs[G1],
        vecs[S1],
        both[:, dim:],
        vecs[UB : UB + times].reshape(-1),
        grad_down,
        vecs[DB],
        vecs[G2],
        vecs[S2],
    )


def solution(mesh):
    three, two, one = P("dp", "blk", None), P("dp", None), P("dp")
    weights = (two, one, two, two, one, two, one, one, one, two, one, two, one, one, one)
    return jax.shard_map(
        local,
        mesh=mesh,
        in_specs=(three, P("dp", "blk"), three) + weights,
        out_specs=(three, three) + weights,
        check_vma=False,
    )
```

```python
import functools

import jax
import jax.numpy as jnp
from jax import lax
from jax.experimental import pallas as pl
from jax.experimental.pallas import tpu as pltpu
from jax.sharding import PartitionSpec as P

H = 12
DH = 64
VECTOR_ROWS = 32
SUM_ROWS = 32
PAIRS = 3

EPS = 1e-12
NEG = -1e30
ROOT_HALF = 0.7071067811865476
DENSITY = 0.3989422804014327
BF = jnp.bfloat16
F32 = jnp.float32
MIB = 1 << 20

QB, VB, OB, G1, S1, DB, G2, S2, UB = range(9)


def dot(a, b, left, right):
    return lax.dot_general(a, b, (((left,), (right,)), ((), ())), preferred_element_type=F32)


def normalize(rows):
    center = rows - jnp.mean(rows, axis=-1, keepdims=True)
    inverse = lax.rsqrt(jnp.mean(center * center, axis=-1, keepdims=True) + EPS)
    return center * inverse, inverse


def normalize_back(grad, normed, inverse):
    return inverse * (
        grad
        - jnp.mean(grad, axis=-1, keepdims=True)
        - normed * jnp.mean(grad * normed, axis=-1, keepdims=True)
    )


def total(a):
    return jnp.sum(a, axis=0, keepdims=True)


def params(limit=56):
    return pltpu.CompilerParams(vmem_limit_bytes=limit * MIB)


def cost(flops, moved, extra=0):
    return pl.CostEstimate(flops=int(flops), bytes_accessed=int(moved), transcendentals=int(extra))


def held(shape):
    return pl.BlockSpec(shape, lambda *_: (0,) * len(shape), pipeline_mode=pl.Buffered(1))


HELD = pl.BlockSpec(memory_space=pl.ANY)
SCALARS = pl.BlockSpec(memory_space=pltpu.SMEM)


class Links:
    def __init__(self):
        self.nd = lax.axis_size("dp")
        self.nb = lax.axis_size("blk")
        self.bits = self.nb.bit_length() - 1
        self.blk = lax.axis_index("blk")
        self.dp = lax.axis_index("dp")
        n = self.nd
        self.order = list(range(0, n, 2)) + list(range(n - 1, 0, -2))
        place = {d: i for i, d in enumerate(self.order)}
        self.core = self.blk & 1
        self.sign = 1 - 2 * self.core
        self.place = jnp.where(self.dp % 2 == 0, self.dp // 2, n - 1 - self.dp // 2)
        pairs = []
        for d in range(n):
            for b in range(self.nb):
                step = 1 if b % 2 == 0 else -1
                target = self.order[(place[d] + step) % n]
                pairs.append((d * self.nb + b, target * self.nb + b))
        self.pairs = pairs
        far = n // 2
        at = [self.dp]
        at += [self.shard_at(-self.sign * s) for s in range(1, far)]
        at += [self.shard_at(self.sign * s) for s in range(1, far)]
        at += [self.shard_at(far), self.core]
        self.sources = jnp.stack(at).astype(jnp.int32)
        at = [self.shard_at(-self.sign * s) for s in range(1, far)]
        at += [self.shard_at(far)]
        at += [self.shard_at(self.sign * s) for s in range(1, far)]
        at += [self.dp]
        self.targets = jnp.stack(at).astype(jnp.int32)

    def swap(self, a, bit):
        return lax.ppermute(a, "blk", [(i, i ^ (1 << bit)) for i in range(self.nb)])

    def step(self, a):
        return lax.ppermute(a, ("dp", "blk"), self.pairs)

    def shard_at(self, offset):
        n = self.nd
        at = (self.place + offset) % n
        return jnp.where(at < n // 2, 2 * at, 2 * (n - 1 - at) + 1)

    def to_rows(self, a):
        for bit in reversed(range(self.bits)):
            half = a.shape[0] // 2
            mine = (self.blk >> bit) & 1
            keep = lax.dynamic_slice_in_dim(a, mine * half, half, 0)
            send = lax.dynamic_slice_in_dim(a, (1 - mine) * half, half, 0)
            got = self.swap(send, bit)
            yield got
            a = jnp.concatenate([keep, got], axis=1)
        yield a

    def from_rows(self, a):
        for bit in range(self.bits):
            half = a.shape[1] // 2
            mine = (self.blk >> bit) & 1
            keep, got = a[:, :half], self.swap(a[:, half:], bit)
            yield got
            a = jnp.where(
                mine == 0,
                jnp.concatenate([keep, got], 0),
                jnp.concatenate([got, keep], 0),
            )
        yield a

    def gather(self, piece, waits=()):
        n, m = self.nd, piece.shape[0]
        mine, other, now = [], [], piece
        waits = dict(enumerate(waits))
        for i in range(n // 2 - 1):
            if i in waits:
                now = after(now, waits[i])
            now = self.step(now)
            mine.append(now)
            other.append(self.swap(now, 0))
        far = self.step(lax.dynamic_slice_in_dim(now, self.core * (m // 2), m // 2, 0))
        return [piece] + mine + other + [far, self.swap(far, 0)]

    def whole(self, pieces):
        n = self.nd
        out = jnp.zeros((n,) + pieces[0].shape, pieces[0].dtype)
        for i, a in enumerate(pieces[:-2]):
            out = lax.dynamic_update_slice(out, a[None], (self.sources[i], 0, 0))
        a, b = pieces[-2:]
        far = jnp.where(self.core == 0, jnp.concatenate([a, b], 0), jnp.concatenate([b, a], 0))
        return lax.dynamic_update_slice(out, far[None], (self.sources[n - 1], 0, 0))

    def scatter(self, parts):
        n, m = self.nd, parts.shape[1]
        far = n // 2
        pick = lambda i: lax.dynamic_index_in_dim(parts, self.targets[i], 0, keepdims=False)
        got = self.swap(jnp.concatenate([pick(i)[None] for i in range(far)], 0), 0)
        yield got
        keep = [pick(i) for i in range(far - 1, n)]
        halved = lambda a: lax.dynamic_slice_in_dim(a, self.core * (m // 2), m // 2, 0).astype(F32)
        acc = halved(keep[0]) + halved(got[far - 1])
        moved = self.step(acc.astype(BF))
        yield moved
        zero = jnp.zeros((m // 2,) + moved.shape[1:], BF)
        moved = jnp.where(
            self.core == 0,
            jnp.concatenate([moved, zero], 0),
            jnp.concatenate([zero, moved], 0),
        )
        for s in range(far - 1, 0, -1):
            acc = keep[s].astype(F32) + got[s - 1].astype(F32) + moved.astype(F32)
            moved = self.step(acc.astype(BF))
            yield moved
        yield from self.total(keep[far].astype(F32) + moved.astype(F32))

    def total(self, acc):
        for bit in range(self.bits):
            low = acc.astype(BF)
            moved = self.swap(low, bit)
            yield moved
            acc = low.astype(F32) + moved.astype(F32)
        yield acc


class Group:
    def __init__(self, arrays, parts, pieces, width):
        self.arrays, self.parts, self.pieces, self.width = arrays, parts, pieces, width

    def shape(self, name):
        mine = [(rows, column) for rows, x, column in self.parts if x == name]
        return (mine[0][0], max(column for _, column in mine) + self.width)

    def place(self, refs, sources, names, into):
        into = dict(zip(names, into))
        n = len(self.arrays) - 1
        half = sum(rows for rows, _, _ in self.parts) // 2
        starts = [sum(p[0] for p in self.parts[:i]) for i in range(len(self.parts))]
        parts = [(start,) + p for start, p in zip(starts, self.parts) if p[1] in names]
        for i in range(n - 1):
            for start, rows, name, column in parts:
                into[name][sources[i], :, column : column + self.width] = refs[i][start : start + rows]
        for core in range(2):

            @pl.when(sources[n] == core)
            def _(core=core):
                for start, rows, name, column in parts:
                    for h in range(2):
                        low, high = max(start, h * half), min(start + rows, (h + 1) * half)
                        if low < high:
                            ref = refs[n - 1] if h == core else refs[n]
                            into[name][
                                sources[n - 1], low - start : high - start, column : column + self.width
                            ] = ref[low - h * half : high - h * half]


def pack(weights, vectors):
    shard, dim = weights[0].shape

    def kernel(*refs):
        mats, vecs, out_ref, table = refs[: len(weights)], refs[len(weights) : -2], refs[-2], refs[-1]
        for i, ref in enumerate(mats):
            out_ref[i * shard : (i + 1) * shard] = ref[...]
        table[...] = jnp.zeros_like(table)
        line = 0
        for ref in vecs:
            a = ref[...].astype(F32)
            for t in range(a.shape[0] // shard):
                table[line : line + 1, :shard] = a[t * shard : (t + 1) * shard].reshape(1, shard)
                line += 1
        blank = jnp.zeros((VECTOR_ROWS, dim - 128), F32)
        out_ref[len(mats) * shard :] = jnp.concatenate([table[...], blank], 1).astype(BF)

    return pl.pallas_call(
        kernel,
        out_shape=jax.ShapeDtypeStruct((len(weights) * shard + VECTOR_ROWS, dim), BF),
        scratch_shapes=[pltpu.VMEM((VECTOR_ROWS, 128), F32)],
        compiler_params=params(),
        cost_estimate=cost(0, 4 * len(weights) * shard * dim),
        name="pack",
    )(*weights, *vectors)


def pack_wide(up, down):
    shard, wide = up.shape
    dim = down.shape[1]

    def kernel(up_ref, down_ref, out_ref):
        for t in range(wide // dim):
            out_ref[t * shard : (t + 1) * shard] = up_ref[:, t * dim : (t + 1) * dim]
        out_ref[wide // dim * shard :] = down_ref[...]

    return pl.pallas_call(
        kernel,
        out_shape=jax.ShapeDtypeStruct((wide // dim * shard + down.shape[0], dim), BF),
        compiler_params=params(),
        cost_estimate=cost(0, 8 * shard * wide),
        name="pack_wide",
    )(up, down)


def after(a, *others):
    return lax.optimization_barrier((a,) + others)[0]


def lay(links, group, names, spread=None):
    n = links.nd
    k = len(group.arrays)
    whole = [group.shape(name) for name in names]
    if not group.pieces:
        out = [a.reshape(n * rows, wide) for a, (rows, wide) in zip(group.arrays, whole)]
        if spread is not None:
            lines = out[-1].reshape(n, VECTOR_ROWS, -1)[:, :, :128].transpose(1, 0, 2)
            out[-1] = dot(lines.reshape(VECTOR_ROWS, n * 128), spread, 1, 0)
        return out
    tables = 0 if spread is None else 1

    def kernel(*refs):
        sources, pieces = refs[0], refs[1 : 1 + k]
        refs = refs[1 + k :]
        outs = refs[tables : tables + len(names)]
        if tables:
            outs = outs[:-1] + (refs[-1],)
        group.place(pieces, sources, names, outs)
        if tables:
            lines = refs[-1][...].astype(F32)[:, :, :128]
            wide = jnp.concatenate([lines[j] for j in range(n)], 1).astype(BF)
            refs[len(names)][...] = dot(wide, refs[0][...], 1, 0)

    out_shape = [jax.ShapeDtypeStruct((n,) + x, BF) for x in whole]
    args, scratch = [links.sources, *group.arrays], []
    specs = [SCALARS] + [held(a.shape) for a in group.arrays]
    if tables:
        args.append(spread)
        specs.append(held(spread.shape))
        out_shape[-1] = jax.ShapeDtypeStruct((VECTOR_ROWS, group.width), F32)
        scratch.append(pltpu.VMEM((n,) + whole[-1], BF))
    out = pl.pallas_call(
        kernel,
        grid=(1,),
        in_specs=specs,
        out_specs=[held(x.shape) for x in out_shape],
        out_shape=out_shape,
        scratch_shapes=scratch,
        compiler_params=params(),
        cost_estimate=cost(0, sum(4 * x.size for x in out_shape)),
        name="lay",
    )(*args)
    return [x.reshape(-1, x.shape[-1]) for x in out]


def head_masks(width):
    lane = lax.broadcasted_iota(jnp.int32, (1, width), 1)
    return [lane // DH == h for h in range(width // DH)]


def fill_bias(bias, down_ref, across_ref):
    bias[...] = jnp.where(down_ref[...][:, :1] == across_ref[0], 0.0, NEG)


def attend(q, k, v, down, across):
    rows, _, length = across.shape
    dim = q.shape[1]
    wide = 128 * PAIRS

    def kernel(down_ref, across_ref, q_ref, k_ref, v_ref, o_ref, log_ref, bias):
        @pl.when(pl.program_id(1) == 0)
        def _():
            fill_bias(bias, down_ref, across_ref)

        masks = head_masks(128)
        for pair in range(PAIRS):
            lanes = slice(128 * pair, 128 * pair + 128)
            scaled = q_ref[:, lanes].astype(F32) * DH**-0.5
            outs = []
            for h, mask in enumerate(masks):
                one = jnp.where(mask, scaled, 0.0).astype(BF)
                s = dot(one, k_ref[:, lanes], 1, 1) + bias[...]
                top = jnp.max(s, axis=1, keepdims=True)
                e = jnp.exp(s - top)
                sums = jnp.sum(e, axis=1, keepdims=True)
                outs.append(dot(e.astype(BF), v_ref[:, lanes], 1, 0) / sums)
                log_ref[0, pair, h, :] = (top + jnp.log(sums))[:, 0]
            o_ref[:, lanes] = jnp.where(masks[0], outs[0], outs[1]).astype(BF)

    block = pl.BlockSpec((length, wide), lambda r, h: (r, h))
    return pl.pallas_call(
        kernel,
        grid=(rows, dim // wide),
        in_specs=[
            pl.BlockSpec((length, 128), lambda r, h: (r, 0)),
            pl.BlockSpec((1, 1, length), lambda r, h: (r, 0, 0)),
            block,
            block,
            block,
        ],
        out_specs=[block, pl.BlockSpec((1, PAIRS, 2, length), lambda r, h: (r, h, 0, 0))],
        out_shape=[
            jax.ShapeDtypeStruct(q.shape, BF),
            jax.ShapeDtypeStruct((rows, dim // 128, 2, length), F32),
        ],
        scratch_shapes=[pltpu.VMEM((length, length), F32)],
        compiler_params=params(),
        cost_estimate=cost(
            16 * rows * H * length * length * DH, 8 * rows * length * dim, rows * H * length * length
        ),
        name="attend",
    )(down, across, q, k, v)


def attend_back(q, k, v, g, logs, down, across, row, grads):
    rows, _, length = across.shape
    dim = q.shape[1]
    wide = 128 * PAIRS
    grads = grads or ()

    def kernel(down_ref, across_ref, q_ref, k_ref, v_ref, g_ref, log_ref, *refs):
        gq_ref, gk_ref, gv_ref, bias = refs[len(grads) :]

        @pl.when(pl.program_id(0) == 0)
        def _():
            fill_bias(bias, down_ref, across_ref)

        masks = head_masks(128)
        for pair in range(PAIRS):
            lanes = slice(128 * pair, 128 * pair + 128)
            keys_t = k_ref[:, lanes].astype(F32).T.astype(BF)
            scaled = q_ref[:, lanes].astype(F32) * DH**-0.5
            scaled_low = scaled.astype(BF)
            grad = g_ref[:, lanes].astype(F32)
            gq, gk, gv = [], [], []
            for h, mask in enumerate(masks):
                one = jnp.where(mask, scaled, 0.0).astype(BF)
                s = dot(k_ref[:, lanes], one, 1, 1) + bias[...]
                p = jnp.exp(s - log_ref[0, pair, h : h + 1, :])
                one = jnp.where(mask, grad, 0.0).astype(BF)
                t = p * dot(v_ref[:, lanes], one, 1, 1)
                gs = (t - p * jnp.sum(t, axis=0, keepdims=True)).astype(BF)
                gv.append(dot(p.astype(BF), g_ref[:, lanes], 1, 0))
                gk.append(dot(gs, scaled_low, 1, 0))
                gq.append(dot(keys_t[h * DH : (h + 1) * DH], gs, 1, 0))
            gq_ref[:, lanes] = (jnp.concatenate(gq, 0).T * DH**-0.5).astype(BF)
            gk_ref[:, lanes] = jnp.where(masks[0], gk[0], gk[1]).astype(BF)
            gv_ref[:, lanes] = jnp.where(masks[0], gv[0], gv[1]).astype(BF)

    block = pl.BlockSpec((length, wide), lambda h: (row, h))
    out = jax.ShapeDtypeStruct(q.shape, BF)
    return pl.pallas_call(
        kernel,
        grid=(dim // wide,),
        in_specs=[
            pl.BlockSpec((length, 128), lambda h: (row, 0)),
            pl.BlockSpec((1, 1, length), lambda h: (row, 0, 0)),
            block,
            block,
            block,
            block,
            pl.BlockSpec((1, PAIRS, 2, length), lambda h: (row, h, 0, 0)),
        ]
        + [HELD] * len(grads),
        out_specs=[block] * 3,
        out_shape=[out] * 3,
        input_output_aliases={7 + i: i for i in range(len(grads))},
        scratch_shapes=[pltpu.VMEM((length, length), F32)],
        compiler_params=params(),
        cost_estimate=cost(
            40 * H * length * length * DH, 14 * length * dim, H * length * length
        ),
        name="attend_back",
    )(down, across, q, k, v, g, logs, *grads)


def share(links, sums, spread, shard):
    n = links.nd
    dim = spread.shape[1]

    def kernel(*refs):
        ins, spread_ref, out_ref, table = refs[: len(sums)], refs[len(sums)], refs[-2], refs[-1]
        table[...] = jnp.zeros_like(table)
        line = 0
        for ref in ins:
            for t in range(ref.shape[0]):
                table[line : line + 1] = ref[t : t + 1]
                line += 1
        low = table[...].astype(BF)
        blank = jnp.zeros((SUM_ROWS, dim - 128), F32)
        for i in range(n):
            part = dot(low, spread_ref[i * 128 : (i + 1) * 128], 1, 1)
            out_ref[i] = jnp.concatenate([part, blank], 1).astype(BF)

    return pl.pallas_call(
        kernel,
        out_shape=jax.ShapeDtypeStruct((n, SUM_ROWS, dim), BF),
        scratch_shapes=[pltpu.VMEM((SUM_ROWS, dim), F32)],
        compiler_params=params(),
        cost_estimate=cost(2 * SUM_ROWS * dim * 128 * n, 4 * SUM_ROWS * dim * n),
        name="share",
    )(*sums, spread)


def local(
    tokens,
    fragments,
    cotangent,
    query_weight,
    query_bias,
    key_weight,
    value_weight,
    value_bias,
    out_weight,
    out_bias,
    first_gain,
    first_shift,
    up_weight,
    up_bias,
    down_weight,
    down_bias,
    second_gain,
    second_shift,
):
    links = Links()
    n = links.nd
    shard, dim = query_weight.shape
    times = up_bias.shape[0] // shard
    aligned = shard % 32 == 0

    vectors = [query_bias, value_bias, out_bias, first_gain, first_shift, down_bias, second_gain, second_shift]
    vectors.append(up_bias)
    piece = pack([query_weight, key_weight, value_weight, out_weight], vectors)
    at = lax.broadcasted_iota(jnp.int32, (n * 128, dim), 0)
    lane = lax.broadcasted_iota(jnp.int32, (n * 128, dim), 1)
    spread = ((at % 128 < shard) & (lane == at // 128 * shard + at % 128)).astype(BF)

    ids_steps = links.to_rows(fragments)
    ids_moved = next(ids_steps)
    x_steps = links.to_rows(after(tokens, ids_moved))
    x_moved = next(x_steps)
    second = after(pack_wide(up_weight, down_weight), piece)
    spread = after(spread, piece)
    first = links.gather(piece, [piece, after(ids_moved, spread), after(x_moved, second)])
    *_, ids = ids_steps
    *_, x = x_steps
    rows, length = ids.shape
    second = links.gather(second, [first[n // 2 - 1]])
    *_, g = links.to_rows(after(cotangent, first[-1]))

    parts = [(shard, name, 0) for name in "qkvo"] + [(VECTOR_ROWS, "vec", 0)]
    if not aligned:
        w = links.whole(first)
        first = [w[:, i * shard : (i + 1) * shard] for i in range(4)] + [w[:, 4 * shard :]]
        w = links.whole(second)
        down_weight = w[:, times * shard :]
        up_weight = w[:, : times * shard].reshape(n, times, shard, dim).transpose(0, 2, 1, 3)
        second = [up_weight, down_weight]
    first = Group(first, parts, aligned, dim)
    parts = [(shard, "u", t * dim) for t in range(times)] + [(times * shard, "d", 0)]
    second = Group(second, parts, aligned, dim)

    x = x.reshape(-1, dim)
    g = g.reshape(-1, dim)
    across = ids[:, None, :]
    down = jnp.broadcast_to(ids.reshape(-1, 1), (rows * length, 128))

    q_w, k_w, v_w, o_w, table = lay(links, first, ["q", "k", "v", "o", "vec"], spread)
    row = lambda i: table[i : i + 1]
    up_row = table[UB : UB + times].reshape(times, n, shard).transpose(1, 0, 2).reshape(1, -1)
    q = (dot(x, q_w, 1, 0) + row(QB)).astype(BF)
    k = dot(x, k_w, 1, 0).astype(BF)
    v = (dot(x, v_w, 1, 0) + row(VB)).astype(BF)
    attended, logs = attend(q, k, v, down, across)
    n1, inv1 = normalize(x.astype(F32) + dot(attended, o_w, 1, 0) + row(OB))
    hidden = n1 * row(G1) + row(S1)
    low = hidden.astype(BF)
    u_w, d_w = lay(links, second, ["u", "d"])
    before = dot(low, u_w, 1, 0) + up_row
    phi = 0.5 * (1.0 + lax.erf(before * ROOT_HALF))
    active = (before * phi).astype(BF)
    slope = (phi + before * (DENSITY * jnp.exp(-0.5 * before * before))).astype(BF)
    n2, inv2 = normalize(hidden + dot(active, d_w, 1, 0) + row(DB))
    result = (n2 * row(G2) + row(S2)).astype(BF)
    grad = g.astype(F32)
    g_r2 = normalize_back(grad * row(G2), n2, inv2)
    g_second = g_r2.astype(BF)
    sums2 = [total(g_second.astype(F32)), total(grad * n2), total(grad)]
    down_steps = links.scatter(dot(active, g_second, 0, 0).astype(BF).reshape(n, -1, dim))
    result_steps = links.from_rows(result.reshape(rows, length, dim))
    g_before = (dot(g_second, d_w, 1, 1) * slope.astype(F32)).astype(BF)
    sums_up = total(g_before.astype(F32))
    g_before = after(g_before, next(down_steps), next(result_steps))
    g_hidden = g_r2 + dot(g_before, u_w, 1, 1)
    g_r1 = normalize_back(g_hidden * row(G1), n1, inv1)
    g_branch = g_r1.astype(BF)
    sums1 = [total(g_branch.astype(F32)), total(g_hidden * n1), total(g_hidden)]
    g_att = dot(g_branch, o_w, 1, 1).astype(BF)
    g_branch = after(g_branch, next(down_steps))
    both = jnp.concatenate([dot(attended, g_branch, 0, 0), dot(low, g_before, 0, 0)], 1)
    up_steps = links.scatter(both.astype(BF).reshape(n, shard, -1))
    g_att = after(g_att, next(down_steps), next(up_steps), next(result_steps))
    grads = attend_back(q, k, v, g_att, logs, down, across, 0, None)
    g_att = after(g_att, next(down_steps), next(up_steps), grads[0])
    gq, gk, gv = attend_back(q, k, v, g_att, logs, down, across, 1, grads)
    gq = after(gq, next(down_steps), next(up_steps))
    up_sums = sums_up[0].reshape(n, times, shard).transpose(1, 0, 2).reshape(times, dim)
    sums = [total(gq.astype(F32)), total(gv.astype(F32))] + sums1 + sums2 + [up_sums]
    each = [dot(x, a, 0, 0).astype(BF).reshape(n, shard, dim) for a in (gq, gk, gv)]
    last_steps = links.scatter(jnp.concatenate(each + [share(links, sums, spread, shard)], 1))
    gk = after(gk, next(down_steps), next(up_steps), next(last_steps))
    g_x = (g_r1 + dot(gq, q_w, 1, 1) + dot(gk, k_w, 1, 1) + dot(gv, v_w, 1, 1)).astype(BF)
    g_x = after(g_x, next(down_steps), next(up_steps), next(last_steps))
    *_, g_x = links.from_rows(g_x.reshape(rows, length, dim))
    *_, result = result_steps
    *_, grad_down = down_steps
    *_, both = up_steps
    *_, last = last_steps
    grad_q, grad_k, grad_v = (last[i * shard : (i + 1) * shard] for i in range(3))
    vecs = last[3 * shard :, :shard]
    return (
        result,
        g_x,
        grad_q,
        vecs[QB],
        grad_k,
        grad_v,
        vecs[VB],
        both[:, :dim],
        vecs[OB],
        vecs[G1],
        vecs[S1],
        both[:, dim:],
        vecs[UB : UB + times].reshape(-1),
        grad_down,
        vecs[DB],
        vecs[G2],
        vecs[S2],
    )


def solution(mesh):
    three, two, one = P("dp", "blk", None), P("dp", None), P("dp")
    weights = (two, one, two, two, one, two, one, one, one, two, one, two, one, one, one)
    return jax.shard_map(
        local,
        mesh=mesh,
        in_specs=(three, P("dp", "blk"), three) + weights,
        out_specs=(three, three) + weights,
        check_vma=False,
    )
```

```python
import functools

import jax
import jax.numpy as jnp
from jax import lax
from jax.experimental import pallas as pl
from jax.experimental.pallas import tpu as pltpu
from jax.sharding import PartitionSpec as P

H = 12
DH = 64
VECTOR_ROWS = 32
SUM_ROWS = 32
PAIRS = 3

EPS = 1e-12
NEG = -1e30
ROOT_HALF = 0.7071067811865476
DENSITY = 0.3989422804014327
BF = jnp.bfloat16
F32 = jnp.float32
MIB = 1 << 20

QB, VB, OB, G1, S1, DB, G2, S2, UB = range(9)


def dot(a, b, left, right):
    return lax.dot_general(a, b, (((left,), (right,)), ((), ())), preferred_element_type=F32)


def normalize(rows):
    center = rows - jnp.mean(rows, axis=-1, keepdims=True)
    inverse = lax.rsqrt(jnp.mean(center * center, axis=-1, keepdims=True) + EPS)
    return center * inverse, inverse


def normalize_back(grad, normed, inverse):
    return inverse * (
        grad
        - jnp.mean(grad, axis=-1, keepdims=True)
        - normed * jnp.mean(grad * normed, axis=-1, keepdims=True)
    )


def total(a):
    return jnp.sum(a, axis=0)


def params(limit=56):
    return pltpu.CompilerParams(vmem_limit_bytes=limit * MIB)


def cost(flops, moved, extra=0):
    return pl.CostEstimate(flops=int(flops), bytes_accessed=int(moved), transcendentals=int(extra))


def held(shape):
    return pl.BlockSpec(shape, lambda *_: (0,) * len(shape), pipeline_mode=pl.Buffered(1))


HELD = pl.BlockSpec(memory_space=pl.ANY)
SCALARS = pl.BlockSpec(memory_space=pltpu.SMEM)


class Links:
    def __init__(self):
        self.nd = lax.axis_size("dp")
        self.nb = lax.axis_size("blk")
        self.bits = self.nb.bit_length() - 1
        self.blk = lax.axis_index("blk")
        self.dp = lax.axis_index("dp")
        n = self.nd
        self.order = list(range(0, n, 2)) + list(range(n - 1, 0, -2))
        place = {d: i for i, d in enumerate(self.order)}
        self.core = self.blk & 1
        self.sign = 1 - 2 * self.core
        self.place = jnp.where(self.dp % 2 == 0, self.dp // 2, n - 1 - self.dp // 2)
        pairs = []
        for d in range(n):
            for b in range(self.nb):
                step = 1 if b % 2 == 0 else -1
                target = self.order[(place[d] + step) % n]
                pairs.append((d * self.nb + b, target * self.nb + b))
        self.pairs = pairs
        far = n // 2
        at = [self.dp]
        at += [self.shard_at(-self.sign * s) for s in range(1, far)]
        at += [self.shard_at(self.sign * s) for s in range(1, far)]
        at += [self.shard_at(far), self.core]
        self.sources = jnp.stack(at).astype(jnp.int32)
        at = [self.shard_at(-self.sign * s) for s in range(1, far)]
        at += [self.shard_at(far)]
        at += [self.shard_at(self.sign * s) for s in range(1, far)]
        at += [self.dp]
        self.targets = jnp.stack(at).astype(jnp.int32)

    def swap(self, a, bit):
        return lax.ppermute(a, "blk", [(i, i ^ (1 << bit)) for i in range(self.nb)])

    def step(self, a):
        return lax.ppermute(a, ("dp", "blk"), self.pairs)

    def shard_at(self, offset):
        n = self.nd
        at = (self.place + offset) % n
        return jnp.where(at < n // 2, 2 * at, 2 * (n - 1 - at) + 1)

    def to_rows(self, a):
        for bit in reversed(range(self.bits)):
            half = a.shape[0] // 2
            mine = (self.blk >> bit) & 1
            keep = lax.dynamic_slice_in_dim(a, mine * half, half, 0)
            send = lax.dynamic_slice_in_dim(a, (1 - mine) * half, half, 0)
            got = yield self.swap(send, bit)
            a = jnp.concatenate([keep, got], axis=1)
        return a

    def from_rows(self, a):
        for bit in range(self.bits):
            half = a.shape[1] // 2
            mine = (self.blk >> bit) & 1
            keep, got = a[:, :half], []
            for part in jnp.split(a[:, half:], min(1 << bit, a.shape[0])):
                got.append((yield self.swap(part, bit)))
            got = jnp.concatenate(got, 0)
            a = jnp.where(
                mine == 0,
                jnp.concatenate([keep, got], 0),
                jnp.concatenate([got, keep], 0),
            )
        return a

    def gather(self, piece):
        n, m = self.nd, piece.shape[0]
        mine, other, now = [], [], piece
        for _ in range(n // 2 - 1):
            now = yield self.step(now)
            mine.append(now)
            other.append(self.swap(now, 0))
        far = yield self.step(lax.dynamic_slice_in_dim(now, self.core * (m // 2), m // 2, 0))
        return [piece] + mine + other + [far, self.swap(far, 0)]

    def whole(self, pieces):
        n = self.nd
        out = jnp.zeros((n,) + pieces[0].shape, pieces[0].dtype)
        for i, a in enumerate(pieces[:-2]):
            out = lax.dynamic_update_slice(out, a[None], (self.sources[i], 0, 0))
        a, b = pieces[-2:]
        far = jnp.where(self.core == 0, jnp.concatenate([a, b], 0), jnp.concatenate([b, a], 0))
        return lax.dynamic_update_slice(out, far[None], (self.sources[n - 1], 0, 0))

    def scatter(self, parts):
        n, m = self.nd, parts.shape[1]
        far = n // 2
        pick = lambda i: lax.dynamic_index_in_dim(parts, self.targets[i], 0, keepdims=False)
        got = yield self.swap(jnp.concatenate([pick(i)[None] for i in range(far)], 0), 0)
        keep = [pick(i) for i in range(far - 1, n)]
        halved = lambda a: lax.dynamic_slice_in_dim(a, self.core * (m // 2), m // 2, 0).astype(F32)
        acc = halved(keep[0]) + halved(got[far - 1])
        moved = yield self.step(acc.astype(BF))
        zero = jnp.zeros((m // 2,) + moved.shape[1:], BF)
        moved = jnp.where(
            self.core == 0,
            jnp.concatenate([moved, zero], 0),
            jnp.concatenate([zero, moved], 0),
        )
        for s in range(far - 1, 0, -1):
            acc = keep[s].astype(F32) + got[s - 1].astype(F32) + moved.astype(F32)
            moved = yield self.step(acc.astype(BF))
        acc = (keep[far].astype(F32) + moved.astype(F32)).astype(BF)
        half = lambda core: lax.dynamic_slice_in_dim(acc, core * (m // 2), m // 2, 0)
        moved = yield self.swap(half(1 - self.core), 0)
        low = (half(self.core).astype(F32) + moved.astype(F32)).astype(BF)
        for bit in range(1, self.bits):
            moved = yield self.swap(low, bit)
            low = (low.astype(F32) + moved.astype(F32)).astype(BF)
        other = yield self.swap(low, 0)
        pair = jnp.where(
            self.core == 0,
            jnp.concatenate([low, other], 0),
            jnp.concatenate([other, low], 0),
        )
        return pair.astype(F32)


class Group:
    def __init__(self, arrays, parts, pieces, width):
        self.arrays, self.parts, self.pieces, self.width = arrays, parts, pieces, width

    def shape(self, name):
        mine = [(rows, column) for rows, x, column in self.parts if x == name]
        return (mine[0][0], max(column for _, column in mine) + self.width)

    def place(self, refs, sources, names, into):
        into = dict(zip(names, into))
        n = len(self.arrays) - 1
        half = sum(rows for rows, _, _ in self.parts) // 2
        starts = [sum(p[0] for p in self.parts[:i]) for i in range(len(self.parts))]
        parts = [(start,) + p for start, p in zip(starts, self.parts) if p[1] in names]
        for i in range(n - 1):
            for start, rows, name, column in parts:
                into[name][sources[i], :, column : column + self.width] = refs[i][start : start + rows]
        for core in range(2):

            @pl.when(sources[n] == core)
            def _(core=core):
                for start, rows, name, column in parts:
                    for h in range(2):
                        low, high = max(start, h * half), min(start + rows, (h + 1) * half)
                        if low < high:
                            ref = refs[n - 1] if h == core else refs[n]
                            into[name][
                                sources[n - 1], low - start : high - start, column : column + self.width
                            ] = ref[low - h * half : high - h * half]


def pack(weights, vectors):
    shard, dim = weights[0].shape

    def kernel(*refs):
        mats, vecs, out_ref, table = refs[: len(weights)], refs[len(weights) : -2], refs[-2], refs[-1]
        for i, ref in enumerate(mats):
            out_ref[i * shard : (i + 1) * shard] = ref[...]
        table[...] = jnp.zeros_like(table)
        line = 0
        for ref in vecs:
            a = ref[...].astype(F32)
            for t in range(a.shape[0] // shard):
                table[line : line + 1, :shard] = a[t * shard : (t + 1) * shard].reshape(1, shard)
                line += 1
        blank = jnp.zeros((VECTOR_ROWS, dim - 128), F32)
        out_ref[len(mats) * shard :] = jnp.concatenate([table[...], blank], 1).astype(BF)

    return pl.pallas_call(
        kernel,
        out_shape=jax.ShapeDtypeStruct((len(weights) * shard + VECTOR_ROWS, dim), BF),
        scratch_shapes=[pltpu.VMEM((VECTOR_ROWS, 128), F32)],
        compiler_params=params(),
        cost_estimate=cost(0, 4 * len(weights) * shard * dim),
        name="pack",
    )(*weights, *vectors)


class Steps:
    def __init__(self, chain):
        self.chain = chain
        self.value = next(chain)
        self.result = None

    def advance(self, value):
        try:
            self.value = self.chain.send(value)
        except StopIteration as end:
            self.value, self.result = None, end.value

    def finish(self):
        while self.value is not None:
            self.advance(self.value)
        return self.result


def beside(a, *chains):
    chains = [c for c in chains if c.value is not None]
    a, values = lax.optimization_barrier((a, tuple(c.value for c in chains)))
    for c, value in zip(chains, values):
        c.advance(value)
    return a


def lay(links, group, names, spread=None):
    n = links.nd
    k = len(group.arrays)
    whole = [group.shape(name) for name in names]
    if not group.pieces:
        out = [a.reshape(n * rows, wide) for a, (rows, wide) in zip(group.arrays, whole)]
        if spread is not None:
            lines = out[-1].reshape(n, VECTOR_ROWS, -1)[:, :, :128].transpose(1, 0, 2)
            out[-1] = dot(lines.reshape(VECTOR_ROWS, n * 128), spread, 1, 0)
        return out
    tables = 0 if spread is None else 1

    def kernel(*refs):
        sources, pieces = refs[0], refs[1 : 1 + k]
        refs = refs[1 + k :]
        outs = refs[tables : tables + len(names)]
        if tables:
            outs = outs[:-1] + (refs[-1],)
        group.place(pieces, sources, names, outs)
        if tables:
            lines = refs[-1][...].astype(F32)[:, :, :128]
            wide = jnp.concatenate([lines[j] for j in range(n)], 1).astype(BF)
            refs[len(names)][...] = dot(wide, refs[0][...], 1, 0)

    out_shape = [jax.ShapeDtypeStruct((n,) + x, BF) for x in whole]
    args, scratch = [links.sources, *group.arrays], []
    specs = [SCALARS] + [held(a.shape) for a in group.arrays]
    if tables:
        args.append(spread)
        specs.append(held(spread.shape))
        out_shape[-1] = jax.ShapeDtypeStruct((VECTOR_ROWS, group.width), F32)
        scratch.append(pltpu.VMEM((n,) + whole[-1], BF))
    out = pl.pallas_call(
        kernel,
        grid=(1,),
        in_specs=specs,
        out_specs=[held(x.shape) for x in out_shape],
        out_shape=out_shape,
        scratch_shapes=scratch,
        compiler_params=params(),
        cost_estimate=cost(0, sum(4 * x.size for x in out_shape)),
        name="lay",
    )(*args)
    return [x.reshape(-1, x.shape[-1]) for x in out]


def head_masks(width):
    lane = lax.broadcasted_iota(jnp.int32, (1, width), 1)
    return [lane // DH == h for h in range(width // DH)]


def fill_bias(bias, down_ref, across_ref):
    bias[...] = jnp.where(down_ref[...][:, :1] == across_ref[0], 0.0, NEG)


def attend(q, k, v, down, across):
    rows, _, length = across.shape
    dim = q.shape[1]
    wide = 128 * PAIRS

    def kernel(down_ref, across_ref, q_ref, k_ref, v_ref, o_ref, log_ref, bias):
        @pl.when(pl.program_id(1) == 0)
        def _():
            fill_bias(bias, down_ref, across_ref)

        masks = head_masks(128)
        for pair in range(PAIRS):
            lanes = slice(128 * pair, 128 * pair + 128)
            scaled = q_ref[:, lanes].astype(F32) * DH**-0.5
            outs = []
            for h, mask in enumerate(masks):
                one = jnp.where(mask, scaled, 0.0).astype(BF)
                s = dot(one, k_ref[:, lanes], 1, 1) + bias[...]
                top = jnp.max(s, axis=1, keepdims=True)
                e = jnp.exp(s - top)
                sums = jnp.sum(e, axis=1, keepdims=True)
                outs.append(dot(e.astype(BF), v_ref[:, lanes], 1, 0) / sums)
                log_ref[0, pair, h, :] = (top + jnp.log(sums))[:, 0]
            o_ref[:, lanes] = jnp.where(masks[0], outs[0], outs[1]).astype(BF)

    block = pl.BlockSpec((length, wide), lambda r, h: (r, h))
    return pl.pallas_call(
        kernel,
        grid=(rows, dim // wide),
        in_specs=[
            pl.BlockSpec((length, 128), lambda r, h: (r, 0)),
            pl.BlockSpec((1, 1, length), lambda r, h: (r, 0, 0)),
            block,
            block,
            block,
        ],
        out_specs=[block, pl.BlockSpec((1, PAIRS, 2, length), lambda r, h: (r, h, 0, 0))],
        out_shape=[
            jax.ShapeDtypeStruct(q.shape, BF),
            jax.ShapeDtypeStruct((rows, dim // 128, 2, length), F32),
        ],
        scratch_shapes=[pltpu.VMEM((length, length), F32)],
        compiler_params=params(),
        cost_estimate=cost(
            16 * rows * H * length * length * DH, 8 * rows * length * dim, rows * H * length * length
        ),
        name="attend",
    )(down, across, q, k, v)


def attend_back(q, k, v, g, logs, down, across, row, grads):
    rows, _, length = across.shape
    dim = q.shape[1]
    wide = 128 * PAIRS
    grads = grads or ()

    def kernel(down_ref, across_ref, q_ref, k_ref, v_ref, g_ref, log_ref, *refs):
        gq_ref, gk_ref, gv_ref, bias = refs[len(grads) :]

        @pl.when(pl.program_id(0) == 0)
        def _():
            fill_bias(bias, down_ref, across_ref)

        masks = head_masks(128)
        for pair in range(PAIRS):
            lanes = slice(128 * pair, 128 * pair + 128)
            keys_t = k_ref[:, lanes].astype(F32).T.astype(BF)
            scaled = q_ref[:, lanes].astype(F32) * DH**-0.5
            scaled_low = scaled.astype(BF)
            grad = g_ref[:, lanes].astype(F32)
            gq, gk, gv = [], [], []
            for h, mask in enumerate(masks):
                one = jnp.where(mask, scaled, 0.0).astype(BF)
                s = dot(k_ref[:, lanes], one, 1, 1) + bias[...]
                p = jnp.exp(s - log_ref[0, pair, h : h + 1, :])
                one = jnp.where(mask, grad, 0.0).astype(BF)
                t = p * dot(v_ref[:, lanes], one, 1, 1)
                gs = (t - p * jnp.sum(t, axis=0, keepdims=True)).astype(BF)
                gv.append(dot(p.astype(BF), g_ref[:, lanes], 1, 0))
                gk.append(dot(gs, scaled_low, 1, 0))
                gq.append(dot(keys_t[h * DH : (h + 1) * DH], gs, 1, 0))
            gq_ref[:, lanes] = (jnp.concatenate(gq, 0).T * DH**-0.5).astype(BF)
            gk_ref[:, lanes] = jnp.where(masks[0], gk[0], gk[1]).astype(BF)
            gv_ref[:, lanes] = jnp.where(masks[0], gv[0], gv[1]).astype(BF)

    block = pl.BlockSpec((length, wide), lambda h: (row, h))
    out = jax.ShapeDtypeStruct(q.shape, BF)
    return pl.pallas_call(
        kernel,
        grid=(dim // wide,),
        in_specs=[
            pl.BlockSpec((length, 128), lambda h: (row, 0)),
            pl.BlockSpec((1, 1, length), lambda h: (row, 0, 0)),
            block,
            block,
            block,
            block,
            pl.BlockSpec((1, PAIRS, 2, length), lambda h: (row, h, 0, 0)),
        ]
        + [HELD] * len(grads),
        out_specs=[block] * 3,
        out_shape=[out] * 3,
        input_output_aliases={7 + i: i for i in range(len(grads))},
        scratch_shapes=[pltpu.VMEM((length, length), F32)],
        compiler_params=params(),
        cost_estimate=cost(
            40 * H * length * length * DH, 14 * length * dim, H * length * length
        ),
        name="attend_back",
    )(down, across, q, k, v, g, logs, *grads)


def share(links, sums, spread, shard):
    n = links.nd
    dim = spread.shape[1]

    def kernel(*refs):
        ins, spread_ref, out_ref, table = refs[: len(sums)], refs[len(sums)], refs[-2], refs[-1]
        table[...] = jnp.zeros_like(table)
        line = 0
        for ref in ins[:-1]:
            table[line : line + 1] = ref[...].reshape(1, dim)
            line += 1
        table[line : line + ins[-1].shape[0]] = ins[-1][...]
        low = table[...].astype(BF)
        blank = jnp.zeros((SUM_ROWS, dim - 128), F32)
        for i in range(n):
            part = dot(low, spread_ref[i * 128 : (i + 1) * 128], 1, 1)
            out_ref[i] = jnp.concatenate([part, blank], 1).astype(BF)

    return pl.pallas_call(
        kernel,
        out_shape=jax.ShapeDtypeStruct((n, SUM_ROWS, dim), BF),
        scratch_shapes=[pltpu.VMEM((SUM_ROWS, dim), F32)],
        compiler_params=params(),
        cost_estimate=cost(2 * SUM_ROWS * dim * 128 * n, 4 * SUM_ROWS * dim * n),
        name="share",
    )(*sums, spread)


def local(
    tokens,
    fragments,
    cotangent,
    query_weight,
    query_bias,
    key_weight,
    value_weight,
    value_bias,
    out_weight,
    out_bias,
    first_gain,
    first_shift,
    up_weight,
    up_bias,
    down_weight,
    down_bias,
    second_gain,
    second_shift,
):
    links = Links()
    n = links.nd
    shard, dim = query_weight.shape
    times = up_bias.shape[0] // shard
    aligned = shard % 32 == 0

    vectors = [query_bias, value_bias, out_bias, first_gain, first_shift, down_bias, second_gain, second_shift]
    vectors.append(up_bias)
    piece = pack([query_weight, key_weight, value_weight, out_weight], vectors)
    at = lax.broadcasted_iota(jnp.int32, (n * 128, dim), 0)
    lane = lax.broadcasted_iota(jnp.int32, (n * 128, dim), 1)
    spread = ((at % 128 < shard) & (lane == at // 128 * shard + at % 128)).astype(BF)

    ids_steps = Steps(links.to_rows(fragments))
    x_steps = Steps(links.to_rows(tokens))
    first = Steps(links.gather(piece))
    first.advance(first.value)
    first.value, spread = lax.optimization_barrier((first.value, spread))
    first.advance(beside(first.value, ids_steps, x_steps))
    up_weight = beside(up_weight, first)
    ups = Steps(links.gather(up_weight))
    first = first.finish()
    ids, x = ids_steps.finish(), x_steps.finish()
    rows, length = ids.shape
    first[0], down_weight = lax.optimization_barrier((beside(first[0], ups), down_weight))
    downs = Steps(links.gather(down_weight))

    parts = [(shard, name, 0) for name in "qkvo"] + [(VECTOR_ROWS, "vec", 0)]
    if not aligned:
        w = links.whole(first)
        first = [w[:, i * shard : (i + 1) * shard] for i in range(4)] + [w[:, 4 * shard :]]
    first = Group(first, parts, aligned, dim)

    def whole(pieces, name, width):
        if not aligned:
            return links.whole(pieces).reshape(-1, width)
        return lay(links, Group(pieces, [(pieces[0].shape[0], name, 0)], True, width), [name])[0]

    x = x.reshape(-1, dim)
    across = ids[:, None, :]
    down = jnp.broadcast_to(ids.reshape(-1, 1), (rows * length, 128))

    q_w, k_w, v_w, o_w, table = lay(links, first, ["q", "k", "v", "o", "vec"], spread)
    row = lambda i: table[i : i + 1]
    up_row = table[UB : UB + times].reshape(times, n, shard).transpose(1, 0, 2).reshape(1, -1)
    q = (dot(x, q_w, 1, 0) + row(QB)).astype(BF)
    k = dot(x, k_w, 1, 0).astype(BF)
    v = (dot(x, v_w, 1, 0) + row(VB)).astype(BF)
    q = beside(q, ups, downs)
    q, cotangent = lax.optimization_barrier((q, cotangent))
    g_steps = Steps(links.to_rows(cotangent))
    attended, logs = attend(q, k, v, down, across)
    attended = beside(attended, ups, downs)
    n1, inv1 = normalize(x.astype(F32) + dot(attended, o_w, 1, 0) + row(OB))
    hidden = n1 * row(G1) + row(S1)
    low = beside(hidden.astype(BF), ups)
    u_w = beside(whole(ups.finish(), "u", times * dim), downs)
    before = dot(low, u_w, 1, 0) + up_row
    phi = 0.5 * (1.0 + lax.erf(before * ROOT_HALF))
    active = (before * phi).astype(BF)
    slope = (phi + before * (DENSITY * jnp.exp(-0.5 * before * before))).astype(BF)
    slope = lax.optimization_barrier(slope)
    active = beside(active, downs, g_steps)
    d_w = whole(downs.finish(), "d", dim)
    n2, inv2 = normalize(hidden + dot(active, d_w, 1, 0) + row(DB))
    result = (n2 * row(G2) + row(S2)).astype(BF)
    grad = g_steps.finish().reshape(-1, dim).astype(F32)
    g_r2 = normalize_back(grad * row(G2), n2, inv2)
    g_second = g_r2.astype(BF)
    sums2 = [total(g_second.astype(F32)), total(grad * n2), total(grad)]
    down_steps = Steps(links.scatter(dot(active, g_second, 0, 0).astype(BF).reshape(n, -1, dim)))
    result_steps = Steps(links.from_rows(result.reshape(rows, length, dim)))
    g_before = (dot(g_second, d_w, 1, 1) * slope.astype(F32)).astype(BF)
    sums_up = total(g_before.astype(F32))
    g_before = beside(g_before, down_steps, result_steps)
    g_hidden = dot(g_before, u_w, 1, 1)
    g_hidden, low = lax.optimization_barrier((g_hidden, low))
    low = beside(low, down_steps)
    grad_up = dot(low, g_before, 0, 0)
    g_hidden = g_r2 + g_hidden
    g_r1 = normalize_back(g_hidden * row(G1), n1, inv1)
    g_branch = g_r1.astype(BF)
    sums1 = [total(g_branch.astype(F32)), total(g_hidden * n1), total(g_hidden)]
    g_att = dot(g_branch, o_w, 1, 1).astype(BF)
    g_branch = beside(g_branch, down_steps)
    both = jnp.concatenate([dot(attended, g_branch, 0, 0), grad_up], 1)
    up_steps = Steps(links.scatter(both.astype(BF).reshape(n, shard, -1)))
    g_att = beside(g_att, down_steps, up_steps)
    grads = list(attend_back(q, k, v, g_att, logs, down, across, 0, None))
    grads, g_att = beside((grads, g_att), down_steps, up_steps, result_steps)
    gq, gk, gv = attend_back(q, k, v, g_att, logs, down, across, 1, grads)
    gq, gk, gv = beside((gq, gk, gv), down_steps, up_steps)
    up_sums = sums_up.reshape(n, times, shard).transpose(1, 0, 2).reshape(times, dim)
    sums = [total(gq.astype(F32)), total(gv.astype(F32))] + sums1 + sums2 + [up_sums]
    each = [dot(x, a, 0, 0).astype(BF).reshape(n, shard, dim) for a in (gq, gk, gv)]
    table = share(links, sums, spread, shard)
    each, table = beside((each, table), up_steps, down_steps)
    cut = (3 * shard + SUM_ROWS) // 2 - shard
    upper = jnp.concatenate([each[0], each[1][:, :cut]], 1)
    lower = jnp.concatenate([each[1][:, cut:], each[2], table], 1)
    upper_steps, lower_steps = (Steps(links.scatter(a)) for a in (upper, lower))
    gq = beside(gq, upper_steps, lower_steps)
    g_x = g_r1 + dot(gq, q_w, 1, 1)
    g_x, gk, gv = beside((g_x, gk, gv), upper_steps, lower_steps)
    g_x = (g_x + dot(gk, k_w, 1, 1) + dot(gv, v_w, 1, 1)).astype(BF)
    g_x_steps = Steps(links.from_rows(g_x.reshape(rows, length, dim)))
    beside((), upper_steps, lower_steps, g_x_steps)
    beside((), upper_steps, lower_steps, g_x_steps, up_steps)
    result = beside(result_steps.value, upper_steps, lower_steps, g_x_steps, up_steps)
    result_steps.advance(result)
    last = jnp.concatenate([upper_steps.finish(), lower_steps.finish()], 0)
    g_x, result, grad_down, both = (a.finish() for a in (g_x_steps, result_steps, down_steps, up_steps))
    grad_q, grad_k, grad_v = (last[i * shard : (i + 1) * shard] for i in range(3))
    vecs = last[3 * shard :, :shard]
    return (
        result,
        g_x,
        grad_q,
        vecs[QB],
        grad_k,
        grad_v,
        vecs[VB],
        both[:, :dim],
        vecs[OB],
        vecs[G1],
        vecs[S1],
        both[:, dim:],
        vecs[UB : UB + times].reshape(-1),
        grad_down,
        vecs[DB],
        vecs[G2],
        vecs[S2],
    )


def solution(mesh):
    three, two, one = P("dp", "blk", None), P("dp", None), P("dp")
    weights = (two, one, two, two, one, two, one, one, one, two, one, two, one, one, one)
    return jax.shard_map(
        local,
        mesh=mesh,
        in_specs=(three, P("dp", "blk"), three) + weights,
        out_specs=(three, three) + weights,
        check_vma=False,
    )
```

```python
import functools

import jax
import jax.numpy as jnp
from jax import lax
from jax.experimental import pallas as pl
from jax.experimental.pallas import tpu as pltpu
from jax.sharding import PartitionSpec as P

H = 12
DH = 64
VECTOR_ROWS = 32
SUM_ROWS = 32
PAIRS = 3
TILE = 256

EPS = 1e-12
NEG = -1e30
ROOT_HALF = 0.7071067811865476
DENSITY = 0.3989422804014327
BF = jnp.bfloat16
F32 = jnp.float32
MIB = 1 << 20

QB, VB, OB, G1, S1, DB, G2, S2, UB = range(9)


def dot(a, b, left, right):
    return lax.dot_general(a, b, (((left,), (right,)), ((), ())), preferred_element_type=F32)


def normalize(rows):
    center = rows - jnp.mean(rows, axis=-1, keepdims=True)
    inverse = lax.rsqrt(jnp.mean(center * center, axis=-1, keepdims=True) + EPS)
    return center * inverse, inverse


def normalize_back(grad, normed, inverse):
    return inverse * (
        grad
        - jnp.mean(grad, axis=-1, keepdims=True)
        - normed * jnp.mean(grad * normed, axis=-1, keepdims=True)
    )


def total(a):
    return jnp.sum(a, axis=0)


def params(limit=56):
    return pltpu.CompilerParams(vmem_limit_bytes=limit * MIB)


def cost(flops, moved, extra=0):
    return pl.CostEstimate(flops=int(flops), bytes_accessed=int(moved), transcendentals=int(extra))


def held(shape):
    return pl.BlockSpec(shape, lambda *_: (0,) * len(shape), pipeline_mode=pl.Buffered(1))


HELD = pl.BlockSpec(memory_space=pl.ANY)
SCALARS = pl.BlockSpec(memory_space=pltpu.SMEM)


class Links:
    def __init__(self):
        self.nd = lax.axis_size("dp")
        self.nb = lax.axis_size("blk")
        self.bits = self.nb.bit_length() - 1
        self.blk = lax.axis_index("blk")
        self.dp = lax.axis_index("dp")
        n = self.nd
        self.order = list(range(0, n, 2)) + list(range(n - 1, 0, -2))
        place = {d: i for i, d in enumerate(self.order)}
        self.core = self.blk & 1
        self.sign = 1 - 2 * self.core
        self.place = jnp.where(self.dp % 2 == 0, self.dp // 2, n - 1 - self.dp // 2)
        pairs = []
        for d in range(n):
            for b in range(self.nb):
                step = 1 if b % 2 == 0 else -1
                target = self.order[(place[d] + step) % n]
                pairs.append((d * self.nb + b, target * self.nb + b))
        self.pairs = pairs
        far = n // 2
        at = [self.dp]
        at += [self.shard_at(-self.sign * s) for s in range(1, far)]
        at += [self.shard_at(self.sign * s) for s in range(1, far)]
        at += [self.shard_at(far), self.core]
        self.sources = jnp.stack(at).astype(jnp.int32)
        at = [self.shard_at(-self.sign * s) for s in range(1, far)]
        at += [self.shard_at(far)]
        at += [self.shard_at(self.sign * s) for s in range(1, far)]
        at += [self.dp]
        self.targets = jnp.stack(at).astype(jnp.int32)

    def swap(self, a, bit):
        return lax.ppermute(a, "blk", [(i, i ^ (1 << bit)) for i in range(self.nb)])

    def step(self, a):
        return lax.ppermute(a, ("dp", "blk"), self.pairs)

    def shard_at(self, offset):
        n = self.nd
        at = (self.place + offset) % n
        return jnp.where(at < n // 2, 2 * at, 2 * (n - 1 - at) + 1)

    def to_rows(self, a):
        for bit in reversed(range(self.bits)):
            half = a.shape[0] // 2
            mine = (self.blk >> bit) & 1
            keep = lax.dynamic_slice_in_dim(a, mine * half, half, 0)
            send = lax.dynamic_slice_in_dim(a, (1 - mine) * half, half, 0)
            got = yield self.swap(send, bit)
            a = jnp.concatenate([keep, got], axis=1)
        return a

    def from_rows(self, a):
        for bit in range(self.bits):
            half = a.shape[1] // 2
            mine = (self.blk >> bit) & 1
            keep, got = a[:, :half], []
            for part in jnp.split(a[:, half:], min(1 << bit, a.shape[0])):
                got.append((yield self.swap(part, bit)))
            got = jnp.concatenate(got, 0)
            a = jnp.where(
                mine == 0,
                jnp.concatenate([keep, got], 0),
                jnp.concatenate([got, keep], 0),
            )
        return a

    def gather(self, piece):
        n, m = self.nd, piece.shape[0]
        mine, other, now = [], [], piece
        for _ in range(n // 2 - 1):
            now = yield self.step(now)
            mine.append(now)
            other.append(self.swap(now, 0))
        far = yield self.step(lax.dynamic_slice_in_dim(now, self.core * (m // 2), m // 2, 0))
        return [piece] + mine + other + [far, self.swap(far, 0)]

    def whole(self, pieces):
        n = self.nd
        out = jnp.zeros((n,) + pieces[0].shape, pieces[0].dtype)
        for i, a in enumerate(pieces[:-2]):
            out = lax.dynamic_update_slice(out, a[None], (self.sources[i], 0, 0))
        a, b = pieces[-2:]
        far = jnp.where(self.core == 0, jnp.concatenate([a, b], 0), jnp.concatenate([b, a], 0))
        return lax.dynamic_update_slice(out, far[None], (self.sources[n - 1], 0, 0))

    def scatter(self, parts):
        n, m = self.nd, parts.shape[1]
        far = n // 2
        pick = lambda i: lax.dynamic_index_in_dim(parts, self.targets[i], 0, keepdims=False)
        got = yield self.swap(jnp.concatenate([pick(i)[None] for i in range(far)], 0), 0)
        keep = [pick(i) for i in range(far - 1, n)]
        halved = lambda a: lax.dynamic_slice_in_dim(a, self.core * (m // 2), m // 2, 0).astype(F32)
        acc = halved(keep[0]) + halved(got[far - 1])
        moved = yield self.step(acc.astype(BF))
        zero = jnp.zeros((m // 2,) + moved.shape[1:], BF)
        moved = jnp.where(
            self.core == 0,
            jnp.concatenate([moved, zero], 0),
            jnp.concatenate([zero, moved], 0),
        )
        for s in range(far - 1, 0, -1):
            acc = keep[s].astype(F32) + got[s - 1].astype(F32) + moved.astype(F32)
            moved = yield self.step(acc.astype(BF))
        acc = (keep[far].astype(F32) + moved.astype(F32)).astype(BF)
        half = lambda core: lax.dynamic_slice_in_dim(acc, core * (m // 2), m // 2, 0)
        moved = yield self.swap(half(1 - self.core), 0)
        low = (half(self.core).astype(F32) + moved.astype(F32)).astype(BF)
        for bit in range(1, self.bits):
            moved = yield self.swap(low, bit)
            low = (low.astype(F32) + moved.astype(F32)).astype(BF)
        other = yield self.swap(low, 0)
        pair = jnp.where(
            self.core == 0,
            jnp.concatenate([low, other], 0),
            jnp.concatenate([other, low], 0),
        )
        return pair.astype(F32)


class Group:
    def __init__(self, arrays, parts, pieces, width):
        self.arrays, self.parts, self.pieces, self.width = arrays, parts, pieces, width

    def shape(self, name):
        mine = [(rows, column) for rows, x, column in self.parts if x == name]
        return (mine[0][0], max(column for _, column in mine) + self.width)

    def place(self, refs, sources, names, into):
        into = dict(zip(names, into))
        n = len(self.arrays) - 1
        half = sum(rows for rows, _, _ in self.parts) // 2
        starts = [sum(p[0] for p in self.parts[:i]) for i in range(len(self.parts))]
        parts = [(start,) + p for start, p in zip(starts, self.parts) if p[1] in names]
        for i in range(n - 1):
            for start, rows, name, column in parts:
                into[name][sources[i], :, column : column + self.width] = refs[i][start : start + rows]
        for core in range(2):

            @pl.when(sources[n] == core)
            def _(core=core):
                for start, rows, name, column in parts:
                    for h in range(2):
                        low, high = max(start, h * half), min(start + rows, (h + 1) * half)
                        if low < high:
                            ref = refs[n - 1] if h == core else refs[n]
                            into[name][
                                sources[n - 1], low - start : high - start, column : column + self.width
                            ] = ref[low - h * half : high - h * half]


def pack(weights, vectors):
    shard, dim = weights[0].shape

    def kernel(*refs):
        mats, vecs, out_ref, table = refs[: len(weights)], refs[len(weights) : -2], refs[-2], refs[-1]
        for i, ref in enumerate(mats):
            out_ref[i * shard : (i + 1) * shard] = ref[...]
        table[...] = jnp.zeros_like(table)
        line = 0
        for ref in vecs:
            a = ref[...].astype(F32)
            for t in range(a.shape[0] // shard):
                table[line : line + 1, :shard] = a[t * shard : (t + 1) * shard].reshape(1, shard)
                line += 1
        blank = jnp.zeros((VECTOR_ROWS, dim - 128), F32)
        out_ref[len(mats) * shard :] = jnp.concatenate([table[...], blank], 1).astype(BF)

    return pl.pallas_call(
        kernel,
        out_shape=jax.ShapeDtypeStruct((len(weights) * shard + VECTOR_ROWS, dim), BF),
        scratch_shapes=[pltpu.VMEM((VECTOR_ROWS, 128), F32)],
        compiler_params=params(),
        cost_estimate=cost(0, 4 * len(weights) * shard * dim),
        name="pack",
    )(*weights, *vectors)


class Steps:
    def __init__(self, chain):
        self.chain = chain
        self.value = next(chain)
        self.result = None

    def advance(self, value):
        try:
            self.value = self.chain.send(value)
        except StopIteration as end:
            self.value, self.result = None, end.value

    def finish(self):
        while self.value is not None:
            self.advance(self.value)
        return self.result


def beside(a, *chains):
    chains = [c for c in chains if c.value is not None]
    a, values = lax.optimization_barrier((a, tuple(c.value for c in chains)))
    for c, value in zip(chains, values):
        c.advance(value)
    return a


def lay(links, group, names, spread=None):
    n = links.nd
    k = len(group.arrays)
    whole = [group.shape(name) for name in names]
    if not group.pieces:
        out = [a.reshape(n * rows, wide) for a, (rows, wide) in zip(group.arrays, whole)]
        if spread is not None:
            lines = out[-1].reshape(n, VECTOR_ROWS, -1)[:, :, :128].transpose(1, 0, 2)
            out[-1] = dot(lines.reshape(VECTOR_ROWS, n * 128), spread, 1, 0)
        return out
    tables = 0 if spread is None else 1

    def kernel(*refs):
        sources, pieces = refs[0], refs[1 : 1 + k]
        refs = refs[1 + k :]
        outs = refs[tables : tables + len(names)]
        if tables:
            outs = outs[:-1] + (refs[-1],)
        group.place(pieces, sources, names, outs)
        if tables:
            lines = refs[-1][...].astype(F32)[:, :, :128]
            wide = jnp.concatenate([lines[j] for j in range(n)], 1).astype(BF)
            refs[len(names)][...] = dot(wide, refs[0][...], 1, 0)

    out_shape = [jax.ShapeDtypeStruct((n,) + x, BF) for x in whole]
    args, scratch = [links.sources, *group.arrays], []
    specs = [SCALARS] + [held(a.shape) for a in group.arrays]
    if tables:
        args.append(spread)
        specs.append(held(spread.shape))
        out_shape[-1] = jax.ShapeDtypeStruct((VECTOR_ROWS, group.width), F32)
        scratch.append(pltpu.VMEM((n,) + whole[-1], BF))
    out = pl.pallas_call(
        kernel,
        grid=(1,),
        in_specs=specs,
        out_specs=[held(x.shape) for x in out_shape],
        out_shape=out_shape,
        scratch_shapes=scratch,
        compiler_params=params(),
        cost_estimate=cost(0, sum(4 * x.size for x in out_shape)),
        name="lay",
    )(*args)
    return [x.reshape(-1, x.shape[-1]) for x in out]


def tiled(width):
    return pl.BlockSpec((TILE, width), lambda i: (i, 0))


def fixed(shape):
    return pl.BlockSpec(shape, lambda *_: (0,) * len(shape))


def hand_over(pairs, sems, first):
    copies = [pltpu.make_async_copy(a, b, sems.at[i]) for i, (a, b) in enumerate(pairs)]

    @pl.when(pl.program_id(0) == (0 if first else pl.num_programs(0) - 1))
    def _():
        for c in copies:
            if first:
                c.start()
            else:
                c.wait()


def project(links, group, x, spread):
    tokens, dim = x.shape
    n = links.nd
    names = ["q", "k", "v", "o", "vec"]
    k = len(group.arrays)
    shapes = [(n,) + group.shape(name) for name in names]

    def kernel(*refs):
        sources, x_ref, spread_ref = refs[:3]
        pieces = refs[3 : 3 + k]
        q_ref, k_ref, v_ref, table_ref, *rest = refs[3 + k :]
        wholes, held_weights, sems = rest[:4], rest[4:9], rest[9]

        @pl.when(pl.program_id(0) == 0)
        def _():
            group.place(pieces, sources, names, held_weights)
            lines = held_weights[4][...].astype(F32)[:, :, :128]
            wide = jnp.concatenate([lines[j] for j in range(n)], 1).astype(BF)
            table_ref[...] = dot(wide, spread_ref[...], 1, 0)

        hand_over(list(zip(held_weights, wholes)), sems, True)
        a = x_ref[...]
        qw, kw, vw = (ref[...].reshape(dim, dim) for ref in held_weights[:3])
        q_ref[...] = (dot(a, qw, 1, 0) + table_ref[QB : QB + 1]).astype(BF)
        k_ref[...] = dot(a, kw, 1, 0).astype(BF)
        v_ref[...] = (dot(a, vw, 1, 0) + table_ref[VB : VB + 1]).astype(BF)
        hand_over(list(zip(held_weights, wholes)), sems, False)

    out = jax.ShapeDtypeStruct((tokens, dim), BF)
    outs = pl.pallas_call(
        kernel,
        grid=(tokens // TILE,),
        in_specs=[SCALARS, tiled(dim), held(spread.shape)] + [held(a.shape) for a in group.arrays],
        out_specs=[tiled(dim)] * 3 + [fixed((VECTOR_ROWS, dim))] + [HELD] * 4,
        out_shape=[out] * 3
        + [jax.ShapeDtypeStruct((VECTOR_ROWS, dim), F32)]
        + [jax.ShapeDtypeStruct(a, BF) for a in shapes[:4]],
        scratch_shapes=[pltpu.VMEM(a, BF) for a in shapes] + [pltpu.SemaphoreType.DMA((4,))],
        compiler_params=params(),
        cost_estimate=cost(6 * tokens * dim * dim, 8 * tokens * dim + 16 * dim * dim),
        name="project",
    )(links.sources, x, spread, *group.arrays)
    return list(outs[:4]) + [a.reshape(dim, dim) for a in outs[4:]]


def contract(links, group, active, n1, g, table):
    tokens, dim = n1.shape
    wide = active.shape[1]
    n = links.nd
    k = len(group.arrays)
    shape = (n,) + group.shape("d")

    def kernel(*refs):
        sources, act_ref, n1_ref, g_ref, table_ref = refs[:5]
        pieces = refs[5 : 5 + k]
        out_ref, gr_ref, gs_ref, sums_ref, whole_ref, dw, sems = refs[5 + k :]

        @pl.when(pl.program_id(0) == 0)
        def _():
            group.place(pieces, sources, ["d"], [dw])
            sums_ref[...] = jnp.zeros_like(sums_ref)

        hand_over([(dw, whole_ref)], sems, True)
        row = lambda i: table_ref[i : i + 1]
        hidden = n1_ref[...] * row(G1) + row(S1)
        second = dot(act_ref[...], dw[...].reshape(wide, dim), 1, 0) + row(DB)
        n2, inv = normalize(hidden + second)
        out_ref[...] = (n2 * row(G2) + row(S2)).astype(BF)
        grad = g_ref[...].astype(F32)
        gr = normalize_back(grad * row(G2), n2, inv)
        gr_ref[...] = gr
        low = gr.astype(BF)
        gs_ref[...] = low
        sums_ref[0:1] += jnp.sum(low.astype(F32), axis=0, keepdims=True)
        sums_ref[1:2] += jnp.sum(grad * n2, axis=0, keepdims=True)
        sums_ref[2:3] += jnp.sum(grad, axis=0, keepdims=True)
        hand_over([(dw, whole_ref)], sems, False)

    outs = pl.pallas_call(
        kernel,
        grid=(tokens // TILE,),
        in_specs=[SCALARS, tiled(wide), tiled(dim), tiled(dim), fixed(table.shape)]
        + [held(a.shape) for a in group.arrays],
        out_specs=[tiled(dim), tiled(dim), tiled(dim), fixed((8, dim)), HELD],
        out_shape=[
            jax.ShapeDtypeStruct((tokens, dim), BF),
            jax.ShapeDtypeStruct((tokens, dim), F32),
            jax.ShapeDtypeStruct((tokens, dim), BF),
            jax.ShapeDtypeStruct((8, dim), F32),
            jax.ShapeDtypeStruct(shape, BF),
        ],
        scratch_shapes=[pltpu.VMEM(shape, BF), pltpu.SemaphoreType.DMA((1,))],
        compiler_params=params(),
        cost_estimate=cost(2 * tokens * dim * wide, tokens * (2 * wide + 14 * dim) + 4 * dim * wide),
        name="contract",
    )(links.sources, active, n1, g, table, *group.arrays)
    result, g_r2, g_second, sums, whole = outs
    return result, g_r2, g_second, [sums[i] for i in range(3)], whole.reshape(wide, dim)


def head_masks(width):
    lane = lax.broadcasted_iota(jnp.int32, (1, width), 1)
    return [lane // DH == h for h in range(width // DH)]


def fill_bias(bias, down_ref, across_ref):
    bias[...] = jnp.where(down_ref[...][:, :1] == across_ref[0], 0.0, NEG)


def attend(q, k, v, down, across):
    rows, _, length = across.shape
    dim = q.shape[1]
    wide = 128 * PAIRS

    def kernel(down_ref, across_ref, q_ref, k_ref, v_ref, o_ref, log_ref, bias):
        @pl.when(pl.program_id(1) == 0)
        def _():
            fill_bias(bias, down_ref, across_ref)

        masks = head_masks(128)
        for pair in range(PAIRS):
            lanes = slice(128 * pair, 128 * pair + 128)
            scaled = q_ref[:, lanes].astype(F32) * DH**-0.5
            outs = []
            for h, mask in enumerate(masks):
                one = jnp.where(mask, scaled, 0.0).astype(BF)
                s = dot(one, k_ref[:, lanes], 1, 1) + bias[...]
                top = jnp.max(s, axis=1, keepdims=True)
                e = jnp.exp(s - top)
                sums = jnp.sum(e, axis=1, keepdims=True)
                outs.append(dot(e.astype(BF), v_ref[:, lanes], 1, 0) / sums)
                log_ref[0, pair, h, :] = (top + jnp.log(sums))[:, 0]
            o_ref[:, lanes] = jnp.where(masks[0], outs[0], outs[1]).astype(BF)

    block = pl.BlockSpec((length, wide), lambda r, h: (r, h))
    return pl.pallas_call(
        kernel,
        grid=(rows, dim // wide),
        in_specs=[
            pl.BlockSpec((length, 128), lambda r, h: (r, 0)),
            pl.BlockSpec((1, 1, length), lambda r, h: (r, 0, 0)),
            block,
            block,
            block,
        ],
        out_specs=[block, pl.BlockSpec((1, PAIRS, 2, length), lambda r, h: (r, h, 0, 0))],
        out_shape=[
            jax.ShapeDtypeStruct(q.shape, BF),
            jax.ShapeDtypeStruct((rows, dim // 128, 2, length), F32),
        ],
        scratch_shapes=[pltpu.VMEM((length, length), F32)],
        compiler_params=params(),
        cost_estimate=cost(
            16 * rows * H * length * length * DH, 8 * rows * length * dim, rows * H * length * length
        ),
        name="attend",
    )(down, across, q, k, v)


def attend_back(q, k, v, g, logs, down, across, row, grads):
    rows, _, length = across.shape
    dim = q.shape[1]
    wide = 128 * PAIRS
    grads = grads or ()

    def kernel(down_ref, across_ref, q_ref, k_ref, v_ref, g_ref, log_ref, *refs):
        gq_ref, gk_ref, gv_ref, bias = refs[len(grads) :]

        @pl.when(pl.program_id(0) == 0)
        def _():
            fill_bias(bias, down_ref, across_ref)

        masks = head_masks(128)
        for pair in range(PAIRS):
            lanes = slice(128 * pair, 128 * pair + 128)
            keys_t = k_ref[:, lanes].astype(F32).T.astype(BF)
            scaled = q_ref[:, lanes].astype(F32) * DH**-0.5
            scaled_low = scaled.astype(BF)
            grad = g_ref[:, lanes].astype(F32)
            gq, gk, gv = [], [], []
            for h, mask in enumerate(masks):
                one = jnp.where(mask, scaled, 0.0).astype(BF)
                s = dot(k_ref[:, lanes], one, 1, 1) + bias[...]
                p = jnp.exp(s - log_ref[0, pair, h : h + 1, :])
                one = jnp.where(mask, grad, 0.0).astype(BF)
                t = p * dot(v_ref[:, lanes], one, 1, 1)
                gs = (t - p * jnp.sum(t, axis=0, keepdims=True)).astype(BF)
                gv.append(dot(p.astype(BF), g_ref[:, lanes], 1, 0))
                gk.append(dot(gs, scaled_low, 1, 0))
                gq.append(dot(keys_t[h * DH : (h + 1) * DH], gs, 1, 0))
            gq_ref[:, lanes] = (jnp.concatenate(gq, 0).T * DH**-0.5).astype(BF)
            gk_ref[:, lanes] = jnp.where(masks[0], gk[0], gk[1]).astype(BF)
            gv_ref[:, lanes] = jnp.where(masks[0], gv[0], gv[1]).astype(BF)

    block = pl.BlockSpec((length, wide), lambda h: (row, h))
    out = jax.ShapeDtypeStruct(q.shape, BF)
    return pl.pallas_call(
        kernel,
        grid=(dim // wide,),
        in_specs=[
            pl.BlockSpec((length, 128), lambda h: (row, 0)),
            pl.BlockSpec((1, 1, length), lambda h: (row, 0, 0)),
            block,
            block,
            block,
            block,
            pl.BlockSpec((1, PAIRS, 2, length), lambda h: (row, h, 0, 0)),
        ]
        + [HELD] * len(grads),
        out_specs=[block] * 3,
        out_shape=[out] * 3,
        input_output_aliases={7 + i: i for i in range(len(grads))},
        scratch_shapes=[pltpu.VMEM((length, length), F32)],
        compiler_params=params(),
        cost_estimate=cost(
            40 * H * length * length * DH, 14 * length * dim, H * length * length
        ),
        name="attend_back",
    )(down, across, q, k, v, g, logs, *grads)


def share(links, sums, spread, shard):
    n = links.nd
    dim = spread.shape[1]

    def kernel(*refs):
        ins, spread_ref, out_ref, table = refs[: len(sums)], refs[len(sums)], refs[-2], refs[-1]
        table[...] = jnp.zeros_like(table)
        line = 0
        for ref in ins[:-1]:
            table[line : line + 1] = ref[...].reshape(1, dim)
            line += 1
        table[line : line + ins[-1].shape[0]] = ins[-1][...]
        low = table[...].astype(BF)
        blank = jnp.zeros((SUM_ROWS, dim - 128), F32)
        for i in range(n):
            part = dot(low, spread_ref[i * 128 : (i + 1) * 128], 1, 1)
            out_ref[i] = jnp.concatenate([part, blank], 1).astype(BF)

    return pl.pallas_call(
        kernel,
        out_shape=jax.ShapeDtypeStruct((n, SUM_ROWS, dim), BF),
        scratch_shapes=[pltpu.VMEM((SUM_ROWS, dim), F32)],
        compiler_params=params(),
        cost_estimate=cost(2 * SUM_ROWS * dim * 128 * n, 4 * SUM_ROWS * dim * n),
        name="share",
    )(*sums, spread)


def local(
    tokens,
    fragments,
    cotangent,
    query_weight,
    query_bias,
    key_weight,
    value_weight,
    value_bias,
    out_weight,
    out_bias,
    first_gain,
    first_shift,
    up_weight,
    up_bias,
    down_weight,
    down_bias,
    second_gain,
    second_shift,
):
    links = Links()
    n = links.nd
    shard, dim = query_weight.shape
    times = up_bias.shape[0] // shard
    aligned = shard % 32 == 0

    vectors = [query_bias, value_bias, out_bias, first_gain, first_shift, down_bias, second_gain, second_shift]
    vectors.append(up_bias)
    piece = pack([query_weight, key_weight, value_weight, out_weight], vectors)
    at = lax.broadcasted_iota(jnp.int32, (n * 128, dim), 0)
    lane = lax.broadcasted_iota(jnp.int32, (n * 128, dim), 1)
    spread = ((at % 128 < shard) & (lane == at // 128 * shard + at % 128)).astype(BF)

    ids_steps = Steps(links.to_rows(fragments))
    x_steps = Steps(links.to_rows(tokens))
    first = Steps(links.gather(piece))
    first.advance(first.value)
    first.value, spread = lax.optimization_barrier((first.value, spread))
    first.advance(beside(first.value, ids_steps, x_steps))
    up_weight = beside(up_weight, first)
    ups = Steps(links.gather(up_weight))
    first = first.finish()
    ids, x = ids_steps.finish(), x_steps.finish()
    rows, length = ids.shape
    first[0], down_weight = lax.optimization_barrier((beside(first[0], ups), down_weight))
    downs = Steps(links.gather(down_weight))

    parts = [(shard, name, 0) for name in "qkvo"] + [(VECTOR_ROWS, "vec", 0)]
    if not aligned:
        w = links.whole(first)
        first = [w[:, i * shard : (i + 1) * shard] for i in range(4)] + [w[:, 4 * shard :]]
    first = Group(first, parts, aligned, dim)

    def whole(pieces, name, width):
        if not aligned:
            return links.whole(pieces).reshape(-1, width)
        return lay(links, Group(pieces, [(pieces[0].shape[0], name, 0)], True, width), [name])[0]

    x = x.reshape(-1, dim)
    across = ids[:, None, :]
    down = jnp.broadcast_to(ids.reshape(-1, 1), (rows * length, 128))

    row = lambda i: table[i : i + 1]
    if aligned:
        q, k, v, table, q_w, k_w, v_w, o_w = project(links, first, x, spread)
    else:
        q_w, k_w, v_w, o_w, table = lay(links, first, ["q", "k", "v", "o", "vec"], spread)
        q = (dot(x, q_w, 1, 0) + row(QB)).astype(BF)
        k = dot(x, k_w, 1, 0).astype(BF)
        v = (dot(x, v_w, 1, 0) + row(VB)).astype(BF)
    up_row = table[UB : UB + times].reshape(times, n, shard).transpose(1, 0, 2).reshape(1, -1)
    q = beside(q, ups, downs)
    q, cotangent = lax.optimization_barrier((q, cotangent))
    g_steps = Steps(links.to_rows(cotangent))
    attended, logs = attend(q, k, v, down, across)
    attended = beside(attended, ups, downs)
    n1, inv1 = normalize(x.astype(F32) + dot(attended, o_w, 1, 0) + row(OB))
    hidden = n1 * row(G1) + row(S1)
    low = beside(hidden.astype(BF), ups)
    u_w = beside(whole(ups.finish(), "u", times * dim), downs)
    before = dot(low, u_w, 1, 0) + up_row
    phi = 0.5 * (1.0 + lax.erf(before * ROOT_HALF))
    active = (before * phi).astype(BF)
    slope = (phi + before * (DENSITY * jnp.exp(-0.5 * before * before))).astype(BF)
    slope = lax.optimization_barrier(slope)
    active = beside(active, downs, g_steps)
    g = g_steps.finish().reshape(-1, dim)
    if aligned:
        downs = Group(downs.finish(), [(times * shard, "d", 0)], True, dim)
        result, g_r2, g_second, sums2, d_w = contract(links, downs, active, n1, g, table)
    else:
        d_w = whole(downs.finish(), "d", dim)
        n2, inv2 = normalize(hidden + dot(active, d_w, 1, 0) + row(DB))
        result = (n2 * row(G2) + row(S2)).astype(BF)
        grad = g.astype(F32)
        g_r2 = normalize_back(grad * row(G2), n2, inv2)
        g_second = g_r2.astype(BF)
        sums2 = [total(g_second.astype(F32)), total(grad * n2), total(grad)]
    down_steps = Steps(links.scatter(dot(active, g_second, 0, 0).astype(BF).reshape(n, -1, dim)))
    result_steps = Steps(links.from_rows(result.reshape(rows, length, dim)))
    g_before = (dot(g_second, d_w, 1, 1) * slope.astype(F32)).astype(BF)
    sums_up = total(g_before.astype(F32))
    g_before = beside(g_before, down_steps, result_steps)
    g_hidden = dot(g_before, u_w, 1, 1)
    g_hidden, low = lax.optimization_barrier((g_hidden, low))
    grad_up = dot(low, g_before, 0, 0)
    g_hidden = g_r2 + g_hidden
    g_r1 = normalize_back(g_hidden * row(G1), n1, inv1)
    g_branch = g_r1.astype(BF)
    sums1 = [total(g_branch.astype(F32)), total(g_hidden * n1), total(g_hidden)]
    g_att = dot(g_branch, o_w, 1, 1).astype(BF)
    g_branch = beside(g_branch, down_steps)
    both = jnp.concatenate([dot(attended, g_branch, 0, 0), grad_up], 1)
    up_steps = Steps(links.scatter(both.astype(BF).reshape(n, shard, -1)))
    g_att = beside(g_att, down_steps, up_steps)
    grads = list(attend_back(q, k, v, g_att, logs, down, across, 0, None))
    grads, g_att = beside((grads, g_att), down_steps, up_steps, result_steps)
    gq, gk, gv = attend_back(q, k, v, g_att, logs, down, across, 1, grads)
    gq, gk, gv = beside((gq, gk, gv), down_steps, up_steps)
    up_sums = sums_up.reshape(n, times, shard).transpose(1, 0, 2).reshape(times, dim)
    sums = [total(gq.astype(F32)), total(gv.astype(F32))] + sums1 + sums2 + [up_sums]
    each = [dot(x, a, 0, 0).astype(BF).reshape(n, shard, dim) for a in (gq, gk, gv)]
    table = share(links, sums, spread, shard)
    gq, table = lax.optimization_barrier((gq, table))
    g_x = g_r1 + dot(gq, q_w, 1, 1) + dot(gk, k_w, 1, 1) + dot(gv, v_w, 1, 1)
    each, table, g_x = beside((each, table, g_x.astype(BF)), up_steps, down_steps)
    cut = (3 * shard + SUM_ROWS) // 2 - shard
    upper = jnp.concatenate([each[0], each[1][:, :cut]], 1)
    lower = jnp.concatenate([each[1][:, cut:], each[2], table], 1)
    g_x_steps = Steps(links.from_rows(g_x.reshape(rows, length, dim)))
    upper_steps, lower_steps = (Steps(links.scatter(a)) for a in (upper, lower))
    beside((), upper_steps, lower_steps, g_x_steps)
    beside((), upper_steps, lower_steps, down_steps)
    beside((), upper_steps, lower_steps, g_x_steps, up_steps)
    result = beside(result_steps.finish(), upper_steps, lower_steps, g_x_steps, up_steps)
    result, grad_down = beside((result, down_steps.finish()), upper_steps, lower_steps)
    last = jnp.concatenate([upper_steps.finish(), lower_steps.finish()], 0)
    g_x, both = (a.finish() for a in (g_x_steps, up_steps))
    grad_q, grad_k, grad_v = (last[i * shard : (i + 1) * shard] for i in range(3))
    vecs = last[3 * shard :, :shard]
    return (
        result,
        g_x,
        grad_q,
        vecs[QB],
        grad_k,
        grad_v,
        vecs[VB],
        both[:, :dim],
        vecs[OB],
        vecs[G1],
        vecs[S1],
        both[:, dim:],
        vecs[UB : UB + times].reshape(-1),
        grad_down,
        vecs[DB],
        vecs[G2],
        vecs[S2],
    )


def solution(mesh):
    three, two, one = P("dp", "blk", None), P("dp", None), P("dp")
    weights = (two, one, two, two, one, two, one, one, one, two, one, two, one, one, one)
    return jax.shard_map(
        local,
        mesh=mesh,
        in_specs=(three, P("dp", "blk"), three) + weights,
        out_specs=(three, three) + weights,
        check_vma=False,
    )
```

```python
import functools

import jax
import jax.numpy as jnp
from jax import lax
from jax.experimental import pallas as pl
from jax.experimental.pallas import tpu as pltpu
from jax.sharding import PartitionSpec as P

H = 12
DH = 64
VECTOR_ROWS = 32
SUM_ROWS = 32
PAIRS = 3
TILE = 256

EPS = 1e-12
NEG = -1e30
ROOT_HALF = 0.7071067811865476
DENSITY = 0.3989422804014327
BF = jnp.bfloat16
F32 = jnp.float32
MIB = 1 << 20

QB, VB, OB, G1, S1, DB, G2, S2, UB = range(9)


def dot(a, b, left, right):
    return lax.dot_general(a, b, (((left,), (right,)), ((), ())), preferred_element_type=F32)


def normalize(rows):
    center = rows - jnp.mean(rows, axis=-1, keepdims=True)
    inverse = lax.rsqrt(jnp.mean(center * center, axis=-1, keepdims=True) + EPS)
    return center * inverse, inverse


def normalize_back(grad, normed, inverse):
    return inverse * (
        grad
        - jnp.mean(grad, axis=-1, keepdims=True)
        - normed * jnp.mean(grad * normed, axis=-1, keepdims=True)
    )


def total(a):
    return jnp.sum(a, axis=0)


def params(limit=56):
    return pltpu.CompilerParams(vmem_limit_bytes=limit * MIB)


def cost(flops, moved, extra=0):
    return pl.CostEstimate(flops=int(flops), bytes_accessed=int(moved), transcendentals=int(extra))


def held(shape):
    return pl.BlockSpec(shape, lambda *_: (0,) * len(shape), pipeline_mode=pl.Buffered(1))


HELD = pl.BlockSpec(memory_space=pl.ANY)
SCALARS = pl.BlockSpec(memory_space=pltpu.SMEM)


class Links:
    def __init__(self):
        self.nd = lax.axis_size("dp")
        self.nb = lax.axis_size("blk")
        self.bits = self.nb.bit_length() - 1
        self.blk = lax.axis_index("blk")
        self.dp = lax.axis_index("dp")
        n = self.nd
        self.order = list(range(0, n, 2)) + list(range(n - 1, 0, -2))
        place = {d: i for i, d in enumerate(self.order)}
        self.core = self.blk & 1
        self.sign = 1 - 2 * self.core
        self.place = jnp.where(self.dp % 2 == 0, self.dp // 2, n - 1 - self.dp // 2)
        pairs = []
        for d in range(n):
            for b in range(self.nb):
                step = 1 if b % 2 == 0 else -1
                target = self.order[(place[d] + step) % n]
                pairs.append((d * self.nb + b, target * self.nb + b))
        self.pairs = pairs
        far = n // 2
        at = [self.dp]
        at += [self.shard_at(-self.sign * s) for s in range(1, far)]
        at += [self.shard_at(self.sign * s) for s in range(1, far)]
        at += [self.shard_at(far), self.core]
        self.sources = jnp.stack(at).astype(jnp.int32)
        at = [self.shard_at(-self.sign * s) for s in range(1, far)]
        at += [self.shard_at(far)]
        at += [self.shard_at(self.sign * s) for s in range(1, far)]
        at += [self.dp]
        self.targets = jnp.stack(at).astype(jnp.int32)

    def swap(self, a, bit):
        return lax.ppermute(a, "blk", [(i, i ^ (1 << bit)) for i in range(self.nb)])

    def step(self, a):
        return lax.ppermute(a, ("dp", "blk"), self.pairs)

    def shard_at(self, offset):
        n = self.nd
        at = (self.place + offset) % n
        return jnp.where(at < n // 2, 2 * at, 2 * (n - 1 - at) + 1)

    def to_rows(self, a):
        for bit in reversed(range(self.bits)):
            half = a.shape[0] // 2
            mine = (self.blk >> bit) & 1
            keep = lax.dynamic_slice_in_dim(a, mine * half, half, 0)
            send = lax.dynamic_slice_in_dim(a, (1 - mine) * half, half, 0)
            got = yield self.swap(send, bit)
            a = jnp.concatenate([keep, got], axis=1)
        return a

    def from_rows(self, a):
        for bit in range(self.bits):
            half = a.shape[1] // 2
            mine = (self.blk >> bit) & 1
            keep, got = a[:, :half], []
            for part in jnp.split(a[:, half:], min(1 << bit, a.shape[0])):
                got.append((yield self.swap(part, bit)))
            got = jnp.concatenate(got, 0)
            a = jnp.where(
                mine == 0,
                jnp.concatenate([keep, got], 0),
                jnp.concatenate([got, keep], 0),
            )
        return a

    def gather(self, piece):
        n, m = self.nd, piece.shape[0]
        mine, other, now = [], [], piece
        for _ in range(n // 2 - 1):
            now = yield self.step(now)
            mine.append(now)
            other.append(self.swap(now, 0))
        far = yield self.step(lax.dynamic_slice_in_dim(now, self.core * (m // 2), m // 2, 0))
        return [piece] + mine + other + [far, self.swap(far, 0)]

    def whole(self, pieces):
        n = self.nd
        out = jnp.zeros((n,) + pieces[0].shape, pieces[0].dtype)
        for i, a in enumerate(pieces[:-2]):
            out = lax.dynamic_update_slice(out, a[None], (self.sources[i], 0, 0))
        a, b = pieces[-2:]
        far = jnp.where(self.core == 0, jnp.concatenate([a, b], 0), jnp.concatenate([b, a], 0))
        return lax.dynamic_update_slice(out, far[None], (self.sources[n - 1], 0, 0))

    def scatter(self, parts):
        n, m = self.nd, parts.shape[1]
        far = n // 2
        pick = lambda i: lax.dynamic_index_in_dim(parts, self.targets[i], 0, keepdims=False)
        got = yield self.swap(jnp.concatenate([pick(i)[None] for i in range(far)], 0), 0)
        keep = [pick(i) for i in range(far - 1, n)]
        halved = lambda a: lax.dynamic_slice_in_dim(a, self.core * (m // 2), m // 2, 0).astype(F32)
        acc = halved(keep[0]) + halved(got[far - 1])
        moved = yield self.step(acc.astype(BF))
        zero = jnp.zeros((m // 2,) + moved.shape[1:], BF)
        moved = jnp.where(
            self.core == 0,
            jnp.concatenate([moved, zero], 0),
            jnp.concatenate([zero, moved], 0),
        )
        for s in range(far - 1, 0, -1):
            acc = keep[s].astype(F32) + got[s - 1].astype(F32) + moved.astype(F32)
            moved = yield self.step(acc.astype(BF))
        acc = (keep[far].astype(F32) + moved.astype(F32)).astype(BF)
        half = lambda core: lax.dynamic_slice_in_dim(acc, core * (m // 2), m // 2, 0)
        moved = yield self.swap(half(1 - self.core), 0)
        low = (half(self.core).astype(F32) + moved.astype(F32)).astype(BF)
        for bit in range(1, self.bits):
            moved = yield self.swap(low, bit)
            low = (low.astype(F32) + moved.astype(F32)).astype(BF)
        other = yield self.swap(low, 0)
        pair = jnp.where(
            self.core == 0,
            jnp.concatenate([low, other], 0),
            jnp.concatenate([other, low], 0),
        )
        return pair.astype(F32)


class Group:
    def __init__(self, arrays, parts, pieces, width):
        self.arrays, self.parts, self.pieces, self.width = arrays, parts, pieces, width

    def shape(self, name):
        mine = [(rows, column) for rows, x, column in self.parts if x == name]
        return (mine[0][0], max(column for _, column in mine) + self.width)

    def place(self, refs, sources, names, into):
        into = dict(zip(names, into))
        n = len(self.arrays) - 1
        half = sum(rows for rows, _, _ in self.parts) // 2
        starts = [sum(p[0] for p in self.parts[:i]) for i in range(len(self.parts))]
        parts = [(start,) + p for start, p in zip(starts, self.parts) if p[1] in names]
        for i in range(n - 1):
            for start, rows, name, column in parts:
                into[name][sources[i], :, column : column + self.width] = refs[i][start : start + rows]
        for core in range(2):

            @pl.when(sources[n] == core)
            def _(core=core):
                for start, rows, name, column in parts:
                    for h in range(2):
                        low, high = max(start, h * half), min(start + rows, (h + 1) * half)
                        if low < high:
                            ref = refs[n - 1] if h == core else refs[n]
                            into[name][
                                sources[n - 1], low - start : high - start, column : column + self.width
                            ] = ref[low - h * half : high - h * half]


def pack(weights, vectors):
    shard, dim = weights[0].shape

    def kernel(*refs):
        mats, vecs, out_ref, table = refs[: len(weights)], refs[len(weights) : -2], refs[-2], refs[-1]
        for i, ref in enumerate(mats):
            out_ref[i * shard : (i + 1) * shard] = ref[...]
        table[...] = jnp.zeros_like(table)
        line = 0
        for ref in vecs:
            a = ref[...].astype(F32)
            for t in range(a.shape[0] // shard):
                table[line : line + 1, :shard] = a[t * shard : (t + 1) * shard].reshape(1, shard)
                line += 1
        blank = jnp.zeros((VECTOR_ROWS, dim - 128), F32)
        out_ref[len(mats) * shard :] = jnp.concatenate([table[...], blank], 1).astype(BF)

    return pl.pallas_call(
        kernel,
        out_shape=jax.ShapeDtypeStruct((len(weights) * shard + VECTOR_ROWS, dim), BF),
        scratch_shapes=[pltpu.VMEM((VECTOR_ROWS, 128), F32)],
        compiler_params=params(),
        cost_estimate=cost(0, 4 * len(weights) * shard * dim),
        name="pack",
    )(*weights, *vectors)


class Steps:
    def __init__(self, chain):
        self.chain = chain
        self.value = next(chain)
        self.result = None

    def advance(self, value):
        try:
            self.value = self.chain.send(value)
        except StopIteration as end:
            self.value, self.result = None, end.value

    def finish(self):
        while self.value is not None:
            self.advance(self.value)
        return self.result


def beside(a, *chains):
    chains = [c for c in chains if c.value is not None]
    a, values = lax.optimization_barrier((a, tuple(c.value for c in chains)))
    for c, value in zip(chains, values):
        c.advance(value)
    return a


def lay(links, group, names, spread=None):
    n = links.nd
    k = len(group.arrays)
    whole = [group.shape(name) for name in names]
    if not group.pieces:
        out = [a.reshape(n * rows, wide) for a, (rows, wide) in zip(group.arrays, whole)]
        if spread is not None:
            lines = out[-1].reshape(n, VECTOR_ROWS, -1)[:, :, :128].transpose(1, 0, 2)
            out[-1] = dot(lines.reshape(VECTOR_ROWS, n * 128), spread, 1, 0)
        return out
    tables = 0 if spread is None else 1

    def kernel(*refs):
        sources, pieces = refs[0], refs[1 : 1 + k]
        refs = refs[1 + k :]
        outs = refs[tables : tables + len(names)]
        if tables:
            outs = outs[:-1] + (refs[-1],)
        group.place(pieces, sources, names, outs)
        if tables:
            lines = refs[-1][...].astype(F32)[:, :, :128]
            wide = jnp.concatenate([lines[j] for j in range(n)], 1).astype(BF)
            refs[len(names)][...] = dot(wide, refs[0][...], 1, 0)

    out_shape = [jax.ShapeDtypeStruct((n,) + x, BF) for x in whole]
    args, scratch = [links.sources, *group.arrays], []
    specs = [SCALARS] + [held(a.shape) for a in group.arrays]
    if tables:
        args.append(spread)
        specs.append(held(spread.shape))
        out_shape[-1] = jax.ShapeDtypeStruct((VECTOR_ROWS, group.width), F32)
        scratch.append(pltpu.VMEM((n,) + whole[-1], BF))
    out = pl.pallas_call(
        kernel,
        grid=(1,),
        in_specs=specs,
        out_specs=[held(x.shape) for x in out_shape],
        out_shape=out_shape,
        scratch_shapes=scratch,
        compiler_params=params(),
        cost_estimate=cost(0, sum(4 * x.size for x in out_shape)),
        name="lay",
    )(*args)
    return [x.reshape(-1, x.shape[-1]) for x in out]


def tiled(width):
    return pl.BlockSpec((TILE, width), lambda i: (i, 0))


def fixed(shape):
    return pl.BlockSpec(shape, lambda *_: (0,) * len(shape))


def hand_over(pairs, sems, first):
    copies = [pltpu.make_async_copy(a, b, sems.at[i]) for i, (a, b) in enumerate(pairs)]

    @pl.when(pl.program_id(0) == (0 if first else pl.num_programs(0) - 1))
    def _():
        for c in copies:
            if first:
                c.start()
            else:
                c.wait()


def project(links, group, x, spread):
    tokens, dim = x.shape
    n = links.nd
    names = ["q", "k", "v", "o", "vec"]
    k = len(group.arrays)
    shapes = [(n,) + group.shape(name) for name in names]

    def kernel(*refs):
        sources, x_ref, spread_ref = refs[:3]
        pieces = refs[3 : 3 + k]
        q_ref, k_ref, v_ref, table_ref, *rest = refs[3 + k :]
        wholes, held_weights, sems = rest[:4], rest[4:9], rest[9]

        @pl.when(pl.program_id(0) == 0)
        def _():
            group.place(pieces, sources, names, held_weights)
            lines = held_weights[4][...].astype(F32)[:, :, :128]
            wide = jnp.concatenate([lines[j] for j in range(n)], 1).astype(BF)
            table_ref[...] = dot(wide, spread_ref[...], 1, 0)

        hand_over(list(zip(held_weights, wholes)), sems, True)
        a = x_ref[...]
        qw, kw, vw = (ref[...].reshape(dim, dim) for ref in held_weights[:3])
        q_ref[...] = (dot(a, qw, 1, 0) + table_ref[QB : QB + 1]).astype(BF)
        k_ref[...] = dot(a, kw, 1, 0).astype(BF)
        v_ref[...] = (dot(a, vw, 1, 0) + table_ref[VB : VB + 1]).astype(BF)
        hand_over(list(zip(held_weights, wholes)), sems, False)

    out = jax.ShapeDtypeStruct((tokens, dim), BF)
    outs = pl.pallas_call(
        kernel,
        grid=(tokens // TILE,),
        in_specs=[SCALARS, tiled(dim), held(spread.shape)] + [held(a.shape) for a in group.arrays],
        out_specs=[tiled(dim)] * 3 + [fixed((VECTOR_ROWS, dim))] + [HELD] * 4,
        out_shape=[out] * 3
        + [jax.ShapeDtypeStruct((VECTOR_ROWS, dim), F32)]
        + [jax.ShapeDtypeStruct(a, BF) for a in shapes[:4]],
        scratch_shapes=[pltpu.VMEM(a, BF) for a in shapes] + [pltpu.SemaphoreType.DMA((4,))],
        compiler_params=params(),
        cost_estimate=cost(6 * tokens * dim * dim, 8 * tokens * dim + 16 * dim * dim),
        name="project",
    )(links.sources, x, spread, *group.arrays)
    return list(outs[:4]) + [a.reshape(dim, dim) for a in outs[4:]]


def contract(links, group, active, n1, g, table):
    tokens, dim = n1.shape
    wide = active.shape[1]
    n = links.nd
    k = len(group.arrays)
    shape = (n,) + group.shape("d")

    def kernel(*refs):
        sources, act_ref, n1_ref, g_ref, table_ref = refs[:5]
        pieces = refs[5 : 5 + k]
        out_ref, gr_ref, gs_ref, sums_ref, whole_ref, dw, sems = refs[5 + k :]

        @pl.when(pl.program_id(0) == 0)
        def _():
            group.place(pieces, sources, ["d"], [dw])
            sums_ref[...] = jnp.zeros_like(sums_ref)

        hand_over([(dw, whole_ref)], sems, True)
        row = lambda i: table_ref[i : i + 1]
        hidden = n1_ref[...] * row(G1) + row(S1)
        second = dot(act_ref[...], dw[...].reshape(wide, dim), 1, 0) + row(DB)
        n2, inv = normalize(hidden + second)
        out_ref[...] = (n2 * row(G2) + row(S2)).astype(BF)
        grad = g_ref[...].astype(F32)
        gr = normalize_back(grad * row(G2), n2, inv)
        gr_ref[...] = gr
        low = gr.astype(BF)
        gs_ref[...] = low
        sums_ref[0:1] += jnp.sum(low.astype(F32), axis=0, keepdims=True)
        sums_ref[1:2] += jnp.sum(grad * n2, axis=0, keepdims=True)
        sums_ref[2:3] += jnp.sum(grad, axis=0, keepdims=True)
        hand_over([(dw, whole_ref)], sems, False)

    outs = pl.pallas_call(
        kernel,
        grid=(tokens // TILE,),
        in_specs=[SCALARS, tiled(wide), tiled(dim), tiled(dim), fixed(table.shape)]
        + [held(a.shape) for a in group.arrays],
        out_specs=[tiled(dim), tiled(dim), tiled(dim), fixed((8, dim)), HELD],
        out_shape=[
            jax.ShapeDtypeStruct((tokens, dim), BF),
            jax.ShapeDtypeStruct((tokens, dim), F32),
            jax.ShapeDtypeStruct((tokens, dim), BF),
            jax.ShapeDtypeStruct((8, dim), F32),
            jax.ShapeDtypeStruct(shape, BF),
        ],
        scratch_shapes=[pltpu.VMEM(shape, BF), pltpu.SemaphoreType.DMA((1,))],
        compiler_params=params(),
        cost_estimate=cost(2 * tokens * dim * wide, tokens * (2 * wide + 14 * dim) + 4 * dim * wide),
        name="contract",
    )(links.sources, active, n1, g, table, *group.arrays)
    result, g_r2, g_second, sums, whole = outs
    return result, g_r2, g_second, [sums[i] for i in range(3)], whole.reshape(wide, dim)


def head_masks(width):
    lane = lax.broadcasted_iota(jnp.int32, (1, width), 1)
    return [lane // DH == h for h in range(width // DH)]


def fill_bias(bias, down_ref, across_ref):
    bias[...] = jnp.where(down_ref[...][:, :1] == across_ref[0], 0.0, NEG)


def attend(q, k, v, down, across):
    rows, _, length = across.shape
    dim = q.shape[1]
    wide = 128 * PAIRS

    def kernel(down_ref, across_ref, q_ref, k_ref, v_ref, o_ref, log_ref, bias):
        @pl.when(pl.program_id(1) == 0)
        def _():
            fill_bias(bias, down_ref, across_ref)

        masks = head_masks(128)
        for pair in range(PAIRS):
            lanes = slice(128 * pair, 128 * pair + 128)
            scaled = q_ref[:, lanes].astype(F32) * DH**-0.5
            outs = []
            for h, mask in enumerate(masks):
                one = jnp.where(mask, scaled, 0.0).astype(BF)
                s = dot(one, k_ref[:, lanes], 1, 1) + bias[...]
                top = jnp.max(s, axis=1, keepdims=True)
                e = jnp.exp(s - top)
                sums = jnp.sum(e, axis=1, keepdims=True)
                outs.append(dot(e.astype(BF), v_ref[:, lanes], 1, 0) / sums)
                log_ref[0, pair, h, :] = (top + jnp.log(sums))[:, 0]
            o_ref[:, lanes] = jnp.where(masks[0], outs[0], outs[1]).astype(BF)

    block = pl.BlockSpec((length, wide), lambda r, h: (r, h))
    return pl.pallas_call(
        kernel,
        grid=(rows, dim // wide),
        in_specs=[
            pl.BlockSpec((length, 128), lambda r, h: (r, 0)),
            pl.BlockSpec((1, 1, length), lambda r, h: (r, 0, 0)),
            block,
            block,
            block,
        ],
        out_specs=[block, pl.BlockSpec((1, PAIRS, 2, length), lambda r, h: (r, h, 0, 0))],
        out_shape=[
            jax.ShapeDtypeStruct(q.shape, BF),
            jax.ShapeDtypeStruct((rows, dim // 128, 2, length), F32),
        ],
        scratch_shapes=[pltpu.VMEM((length, length), F32)],
        compiler_params=params(),
        cost_estimate=cost(
            16 * rows * H * length * length * DH, 8 * rows * length * dim, rows * H * length * length
        ),
        name="attend",
    )(down, across, q, k, v)


def attend_back(q, k, v, g, logs, down, across, row, grads):
    rows, _, length = across.shape
    dim = q.shape[1]
    wide = 128 * PAIRS
    grads = grads or ()

    def kernel(down_ref, across_ref, q_ref, k_ref, v_ref, g_ref, log_ref, *refs):
        gq_ref, gk_ref, gv_ref, bias = refs[len(grads) :]

        @pl.when(pl.program_id(0) == 0)
        def _():
            fill_bias(bias, down_ref, across_ref)

        masks = head_masks(128)
        for pair in range(PAIRS):
            lanes = slice(128 * pair, 128 * pair + 128)
            keys_t = k_ref[:, lanes].astype(F32).T.astype(BF)
            scaled = q_ref[:, lanes].astype(F32) * DH**-0.5
            scaled_low = scaled.astype(BF)
            grad = g_ref[:, lanes].astype(F32)
            gq, gk, gv = [], [], []
            for h, mask in enumerate(masks):
                one = jnp.where(mask, scaled, 0.0).astype(BF)
                s = dot(k_ref[:, lanes], one, 1, 1) + bias[...]
                p = jnp.exp(s - log_ref[0, pair, h : h + 1, :])
                one = jnp.where(mask, grad, 0.0).astype(BF)
                t = p * dot(v_ref[:, lanes], one, 1, 1)
                gs = (t - p * jnp.sum(t, axis=0, keepdims=True)).astype(BF)
                gv.append(dot(p.astype(BF), g_ref[:, lanes], 1, 0))
                gk.append(dot(gs, scaled_low, 1, 0))
                gq.append(dot(keys_t[h * DH : (h + 1) * DH], gs, 1, 0))
            gq_ref[:, lanes] = (jnp.concatenate(gq, 0).T * DH**-0.5).astype(BF)
            gk_ref[:, lanes] = jnp.where(masks[0], gk[0], gk[1]).astype(BF)
            gv_ref[:, lanes] = jnp.where(masks[0], gv[0], gv[1]).astype(BF)

    block = pl.BlockSpec((length, wide), lambda h: (row, h))
    out = jax.ShapeDtypeStruct(q.shape, BF)
    return pl.pallas_call(
        kernel,
        grid=(dim // wide,),
        in_specs=[
            pl.BlockSpec((length, 128), lambda h: (row, 0)),
            pl.BlockSpec((1, 1, length), lambda h: (row, 0, 0)),
            block,
            block,
            block,
            block,
            pl.BlockSpec((1, PAIRS, 2, length), lambda h: (row, h, 0, 0)),
        ]
        + [HELD] * len(grads),
        out_specs=[block] * 3,
        out_shape=[out] * 3,
        input_output_aliases={7 + i: i for i in range(len(grads))},
        scratch_shapes=[pltpu.VMEM((length, length), F32)],
        compiler_params=params(),
        cost_estimate=cost(
            40 * H * length * length * DH, 14 * length * dim, H * length * length
        ),
        name="attend_back",
    )(down, across, q, k, v, g, logs, *grads)


def share(links, sums, spread, shard):
    n = links.nd
    dim = spread.shape[1]

    def kernel(*refs):
        ins, spread_ref, out_ref, table = refs[: len(sums)], refs[len(sums)], refs[-2], refs[-1]
        table[...] = jnp.zeros_like(table)
        line = 0
        for ref in ins[:-1]:
            table[line : line + 1] = ref[...].reshape(1, dim)
            line += 1
        table[line : line + ins[-1].shape[0]] = ins[-1][...]
        low = table[...].astype(BF)
        blank = jnp.zeros((SUM_ROWS, dim - 128), F32)
        parts = dot(low, spread_ref[...], 1, 1)
        for i in range(n):
            part = parts[:, i * 128 : (i + 1) * 128]
            out_ref[i] = jnp.concatenate([part, blank], 1).astype(BF)

    return pl.pallas_call(
        kernel,
        out_shape=jax.ShapeDtypeStruct((n, SUM_ROWS, dim), BF),
        scratch_shapes=[pltpu.VMEM((SUM_ROWS, dim), F32)],
        compiler_params=params(),
        cost_estimate=cost(2 * SUM_ROWS * dim * 128 * n, 4 * SUM_ROWS * dim * n),
        name="share",
    )(*sums, spread)


def local(
    tokens,
    fragments,
    cotangent,
    query_weight,
    query_bias,
    key_weight,
    value_weight,
    value_bias,
    out_weight,
    out_bias,
    first_gain,
    first_shift,
    up_weight,
    up_bias,
    down_weight,
    down_bias,
    second_gain,
    second_shift,
):
    links = Links()
    n = links.nd
    shard, dim = query_weight.shape
    times = up_bias.shape[0] // shard
    aligned = shard % 32 == 0

    vectors = [query_bias, value_bias, out_bias, first_gain, first_shift, down_bias, second_gain, second_shift]
    vectors.append(up_bias)
    piece = pack([query_weight, key_weight, value_weight, out_weight], vectors)
    at = lax.broadcasted_iota(jnp.int32, (n * 128, dim), 0)
    lane = lax.broadcasted_iota(jnp.int32, (n * 128, dim), 1)
    spread = ((at % 128 < shard) & (lane == at // 128 * shard + at % 128)).astype(BF)

    ids_steps = Steps(links.to_rows(fragments))
    x_steps = Steps(links.to_rows(tokens))
    first = Steps(links.gather(piece))
    first.advance(first.value)
    first.value, spread = lax.optimization_barrier((first.value, spread))
    first.advance(beside(first.value, ids_steps, x_steps))
    up_weight = beside(up_weight, first)
    ups = Steps(links.gather(up_weight))
    first = first.finish()
    ids, x = ids_steps.finish(), x_steps.finish()
    rows, length = ids.shape
    first[0], down_weight = lax.optimization_barrier((beside(first[0], ups), down_weight))
    downs = Steps(links.gather(down_weight))

    parts = [(shard, name, 0) for name in "qkvo"] + [(VECTOR_ROWS, "vec", 0)]
    if not aligned:
        w = links.whole(first)
        first = [w[:, i * shard : (i + 1) * shard] for i in range(4)] + [w[:, 4 * shard :]]
    first = Group(first, parts, aligned, dim)

    def whole(pieces, name, width):
        if not aligned:
            return links.whole(pieces).reshape(-1, width)
        return lay(links, Group(pieces, [(pieces[0].shape[0], name, 0)], True, width), [name])[0]

    x = x.reshape(-1, dim)
    across = ids[:, None, :]
    down = jnp.broadcast_to(ids.reshape(-1, 1), (rows * length, 128))

    row = lambda i: table[i : i + 1]
    if aligned:
        q, k, v, table, q_w, k_w, v_w, o_w = project(links, first, x, spread)
    else:
        q_w, k_w, v_w, o_w, table = lay(links, first, ["q", "k", "v", "o", "vec"], spread)
        q = (dot(x, q_w, 1, 0) + row(QB)).astype(BF)
        k = dot(x, k_w, 1, 0).astype(BF)
        v = (dot(x, v_w, 1, 0) + row(VB)).astype(BF)
    up_row = table[UB : UB + times].reshape(times, n, shard).transpose(1, 0, 2).reshape(1, -1)
    q = beside(q, ups, downs)
    q, cotangent = lax.optimization_barrier((q, cotangent))
    g_steps = Steps(links.to_rows(cotangent))
    attended, logs = attend(q, k, v, down, across)
    attended = beside(attended, ups, downs)
    n1, inv1 = normalize(x.astype(F32) + dot(attended, o_w, 1, 0) + row(OB))
    hidden = n1 * row(G1) + row(S1)
    low = beside(hidden.astype(BF), ups)
    u_w = beside(whole(ups.finish(), "u", times * dim), downs)
    before = dot(low, u_w, 1, 0) + up_row
    phi = 0.5 * (1.0 + lax.erf(before * ROOT_HALF))
    active = (before * phi).astype(BF)
    slope = (phi + before * (DENSITY * jnp.exp(-0.5 * before * before))).astype(BF)
    slope = lax.optimization_barrier(slope)
    active = beside(active, downs, g_steps)
    g = g_steps.finish().reshape(-1, dim)
    if aligned:
        downs = Group(downs.finish(), [(times * shard, "d", 0)], True, dim)
        result, g_r2, g_second, sums2, d_w = contract(links, downs, active, n1, g, table)
    else:
        d_w = whole(downs.finish(), "d", dim)
        n2, inv2 = normalize(hidden + dot(active, d_w, 1, 0) + row(DB))
        result = (n2 * row(G2) + row(S2)).astype(BF)
        grad = g.astype(F32)
        g_r2 = normalize_back(grad * row(G2), n2, inv2)
        g_second = g_r2.astype(BF)
        sums2 = [total(g_second.astype(F32)), total(grad * n2), total(grad)]
    down_steps = Steps(links.scatter(dot(active, g_second, 0, 0).astype(BF).reshape(n, -1, dim)))
    result_steps = Steps(links.from_rows(result.reshape(rows, length, dim)))
    g_before = (dot(g_second, d_w, 1, 1) * slope.astype(F32)).astype(BF)
    sums_up = total(g_before.astype(F32))
    g_before = beside(g_before, down_steps, result_steps)
    g_hidden = dot(g_before, u_w, 1, 1)
    g_hidden, low = lax.optimization_barrier((g_hidden, low))
    grad_up = dot(low, g_before, 0, 0)
    g_hidden = g_r2 + g_hidden
    g_r1 = normalize_back(g_hidden * row(G1), n1, inv1)
    g_branch = g_r1.astype(BF)
    sums1 = [total(g_branch.astype(F32)), total(g_hidden * n1), total(g_hidden)]
    g_att = dot(g_branch, o_w, 1, 1).astype(BF)
    g_branch = beside(g_branch, down_steps)
    both = jnp.concatenate([dot(attended, g_branch, 0, 0), grad_up], 1)
    up_steps = Steps(links.scatter(both.astype(BF).reshape(n, shard, -1)))
    g_att = beside(g_att, down_steps, up_steps)
    grads = list(attend_back(q, k, v, g_att, logs, down, across, 0, None))
    grads, g_att = beside((grads, g_att), down_steps, up_steps, result_steps)
    gq, gk, gv = attend_back(q, k, v, g_att, logs, down, across, 1, grads)
    gq, gk, gv = beside((gq, gk, gv), down_steps, up_steps)
    up_sums = sums_up.reshape(n, times, shard).transpose(1, 0, 2).reshape(times, dim)
    sums = [total(gq.astype(F32)), total(gv.astype(F32))] + sums1 + sums2 + [up_sums]
    each = [dot(x, a, 0, 0).astype(BF).reshape(n, shard, dim) for a in (gq, gk, gv)]
    table = share(links, sums, spread, shard)
    gq, table = lax.optimization_barrier((gq, table))
    g_x = g_r1 + dot(gq, q_w, 1, 1) + dot(gk, k_w, 1, 1) + dot(gv, v_w, 1, 1)
    each, table, g_x = beside((each, table, g_x.astype(BF)), up_steps, down_steps)
    cut = (3 * shard + SUM_ROWS) // 2 - shard
    upper = jnp.concatenate([each[0], each[1][:, :cut]], 1)
    lower = jnp.concatenate([each[1][:, cut:], each[2], table], 1)
    g_x_steps = Steps(links.from_rows(g_x.reshape(rows, length, dim)))
    upper_steps, lower_steps = (Steps(links.scatter(a)) for a in (upper, lower))
    beside((), upper_steps, lower_steps, g_x_steps)
    beside((), upper_steps, lower_steps, down_steps)
    beside((), upper_steps, lower_steps, g_x_steps, up_steps)
    result = beside(result_steps.finish(), upper_steps, lower_steps, g_x_steps, up_steps)
    result, grad_down = beside((result, down_steps.finish()), upper_steps, lower_steps)
    lower_steps.advance(lower_steps.value)
    both = up_steps.finish()
    grad_out, grad_up = beside((both[:, :dim], both[:, dim:]), lower_steps)
    last = jnp.concatenate([upper_steps.finish(), lower_steps.finish()], 0)
    g_x = g_x_steps.finish()
    grad_q, grad_k, grad_v = (last[i * shard : (i + 1) * shard] for i in range(3))
    vecs = last[3 * shard :, :shard]
    return (
        result,
        g_x,
        grad_q,
        vecs[QB],
        grad_k,
        grad_v,
        vecs[VB],
        grad_out,
        vecs[OB],
        vecs[G1],
        vecs[S1],
        grad_up,
        vecs[UB : UB + times].reshape(-1),
        grad_down,
        vecs[DB],
        vecs[G2],
        vecs[S2],
    )


def solution(mesh):
    three, two, one = P("dp", "blk", None), P("dp", None), P("dp")
    weights = (two, one, two, two, one, two, one, one, one, two, one, two, one, one, one)
    return jax.shard_map(
        local,
        mesh=mesh,
        in_specs=(three, P("dp", "blk"), three) + weights,
        out_specs=(three, three) + weights,
        check_vma=False,
    )
```
